32 devices in a mesh: row: 4 (over x, core), col: 8 (over z, y).
Axes of the slice: x: 2, y: 2, z: 4, core: 2. Of those that a mesh axis runs over, the one named last changes fastest.
Arguments:
- heights: float32 [1024, 2048], P('row', 'col'), may hold values from -2 to 2
- shadow: int32 [1024, 2048], P('row', 'col'), may hold values 0 or 1
- image_tiles: bfloat16 [2048, 256, 256], P(('row', 'col')), may hold values from 0.019897461 to 0.59765625
- image_dest: int32 [2048, 1], P(('row', 'col')), may hold values from 0 to 31; in each aligned block of 64 rows (0 to 63, 64 to 127, ...) at most 4 rows name the same one
- sun_gain: bfloat16 [2048, 4], P(('row', 'col')), may hold values from -1 to 2.5, as said below
- shot_dest: int32 [8192, 1], P(('row', 'col')), may hold values from 0 to 31; in each aligned block of 256 rows (0 to 255, 256 to 511, ...) at most 16 rows name the same one
- shot_pixel: int32 [8192], P(('row', 'col')), may hold values from 0 to 65535
- shot_height: float32 [8192], P(('row', 'col')), may hold values from -2 to 2
Outputs:
- surface: float32 [1024, 2048], P('row', 'col')
The draws below stay inside these ranges and needn't reach their ends.
Inputs may be any that keep to these rules, and one draw needn't show every extreme that they name: `image_dest`: among one device's 64 image tiles, no tile owner is named more than 4 times. `shot_dest`: among one device's 256 laser shots, no tile owner is named more than 16 times. `sun_gain`: each row is a unit sun direction with elevation between 0.02 and 0.35 radians, followed by a gain between 0.4 and 2.5.
All inputs are finite; a program needn't handle non-finite values. No bound on the sum of `shadow` on one device may be relied on, other than what follows from the above.
Results may differ from the reference program's by a relative error of at most 0.0015.
Values may be sent and summed in bfloat16 or wider, within the bound.
A program may use at most 256 MiB of HBM per device.

```python
import math
import jax
import jax.numpy as jnp
import numpy as np
from jax import lax

TILE = 256
IMG_DEV = 64
SHOT_DEV = 256
ITERS = 2
CAP = 4
SCAP = 16
IMAGES = 2048
SHOTS = 8192
NH = 1024
NW = 2048
N_ROW = 4
N_COL = 8
DEVICES = 32


def draw_sun_gain(key, part):
    key = jax.random.fold_in(key, 7)
    key_a, key_b, key_c = jax.random.split(key, 3)
    azimuth = jax.random.uniform(key_a, (IMAGES,), jnp.float32, -math.pi, math.pi)
    elevation = jnp.exp(jax.random.uniform(key_b, (IMAGES,), jnp.float32, math.log(0.03), math.log(0.3)))
    gain = jnp.exp(jax.random.uniform(key_c, (IMAGES,), jnp.float32, math.log(0.5), math.log(2.0)))
    flat = jnp.cos(elevation)
    table = jnp.stack([flat * jnp.cos(azimuth), flat * jnp.sin(azimuth), jnp.sin(elevation), gain], axis=1)
    return table.astype(jnp.bfloat16)


def set_ends(array, own_key, smallest, largest):
    spot = [jax.random.randint(jax.random.fold_in(own_key, axis), (), 0, length) for axis, length in enumerate(array.shape)]
    longest = array.shape.index(max(array.shape))
    neighbour = spot[:longest] + [(spot[longest] + 1) % array.shape[longest]] + spot[longest + 1:]
    return array.at[tuple(spot)].set(smallest).at[tuple(neighbour)].set(largest)


def block_scale(key, shape, cuts, low, top_value):
    def one(axis_at, parts):
        steps = jax.random.uniform(jax.random.fold_in(jax.random.fold_in(key, 6), axis_at), (parts,), jnp.float32, low / len(cuts), top_value / len(cuts))
        return jnp.repeat(jnp.exp(steps), shape[axis_at] // parts).reshape((-1,) + (1,) * (len(shape) - axis_at - 1))

    level = one(*cuts[0])
    for cut in cuts[1:]:
        level = level * one(*cut)
    return level


def routed_block(key, own, number, rows, count, top, bound, slope):
    sequence = jax.random.permutation(key, count)
    heavy_load, usual = shares(count, rows * top, bound, slope, True), shares(count, rows * top, bound, slope, False)
    places = jnp.arange(count)

    def named(tallies, rotation):
        used = int((tallies > 0).sum())
        fixed = max(1, used // 4)
        passed = fixed + (places - fixed + rotation * (used - fixed)) % max(1, count - fixed)
        return jnp.zeros((count,), jnp.int32).at[sequence[jnp.where(places < fixed, places, passed)]].set(jnp.asarray(tallies, jnp.int32))

    tallies = jnp.where(number % 4 == 0, named(heavy_load, number // 4), named(usual, number - number // 4 - 1))
    mixed = jax.random.permutation(jax.random.fold_in(own, 3), count)
    giver, receiver = mixed[0:count // 2 * 2:2], mixed[1:count // 2 * 2:2]
    margin = jnp.minimum(tallies[giver] - 1, bound - tallies[receiver]) // 2
    margin = jnp.where((giver == sequence[0]) | (receiver == sequence[0]) | (tallies[receiver] == 0), 0, jnp.maximum(margin, 0))
    passed = jax.random.randint(jax.random.fold_in(own, 4), (count // 2,), 0, 1 << 20) % (margin + 1)
    tallies = tallies.at[giver].add(-passed).at[receiver].add(passed)
    members = jnp.searchsorted(jnp.cumsum(tallies), jnp.arange(rows * top), side="right").astype(jnp.int32)
    table = members.reshape(top, rows).T
    table = table[jax.random.permutation(jax.random.fold_in(own, 1), rows)]
    rotation = jax.random.randint(jax.random.fold_in(own, 2), (rows, 1), 0, top)
    return jnp.take_along_axis(table, (jnp.arange(top)[None, :] + rotation) % top, axis=1)


def shares(amount, total, limit, skew, full):
    loads = [(1 << 20) // math.isqrt(standing ** skew) + 1 for standing in range(1, amount + 1)]
    largest = limit if full else min(limit, max(-(-total // amount), total * loads[0] // sum(loads)))
    least = 1 if total - largest >= amount - 1 else 0
    counts, surplus = [largest] + [least] * (amount - 1), total - largest - least * (amount - 1)
    while surplus > 0:
        movable = [i for i in range(1, amount) if counts[i] < largest] or [i for i in range(1, amount) if counts[i] < limit]
        mass, budget = sum([loads[i] for i in movable]), surplus
        for i in movable:
            extra = min(limit - counts[i], max(1, budget * loads[i] // mass), surplus)
            counts[i] = counts[i] + extra
            surplus = surplus - extra
    return np.array(counts)


def normal_values(own_key, extent, width, reach, cuts=(), dtype=jnp.bfloat16):
    drawn = width * jax.random.normal(own_key, extent, jnp.float32)
    if cuts:
        drawn = drawn * block_scale(own_key, extent, cuts, -0.22, 0.18)
    return jnp.clip(drawn, -reach, reach).astype(dtype)


def setup_inputs(seed: int = 0) -> dict:
    key_of = jax.random.split(jax.random.key(seed), 9)
    heights = normal_values(key_of[0], (NH, NW), 0.3, 2.0, ((0, 4), (1, 8)), jnp.float32)
    shadow = set_ends((jax.random.randint(key_of[1], (NH, NW), 0, 8) < 1).astype(jnp.int32), jax.random.fold_in(key_of[1], 1), 0, 1)
    image_tiles = jnp.clip(0.019897461 + 0.5777588 * jax.random.uniform(key_of[2], (IMAGES, TILE, TILE), jnp.float32) ** block_scale(key_of[2], (IMAGES, TILE, TILE), ((0, 32),), -0.2, 0.2), 0.019897461, 0.59765625).astype(jnp.bfloat16)
    image_dest_keys = jax.random.split(jax.random.fold_in(key_of[3], 1), IMAGES // IMG_DEV)
    image_dest_turns = jax.random.permutation(jax.random.fold_in(key_of[3], 3), IMAGES // IMG_DEV)
    image_dest = jax.vmap(lambda own, number: routed_block(jax.random.fold_in(key_of[3], 2), own, number, IMG_DEV, DEVICES, 1, CAP, 2))(image_dest_keys, image_dest_turns).reshape((IMAGES, 1))
    sun_gain = draw_sun_gain(jax.random.fold_in(key_of[8], 71), 0)
    shot_dest_keys = jax.random.split(jax.random.fold_in(key_of[5], 1), SHOTS // SHOT_DEV)
    shot_dest_turns = jax.random.permutation(jax.random.fold_in(key_of[5], 3), SHOTS // SHOT_DEV)
    shot_dest = jax.vmap(lambda own, number: routed_block(jax.random.fold_in(key_of[5], 2), own, number, SHOT_DEV, DEVICES, 1, SCAP, 1))(shot_dest_keys, shot_dest_turns).reshape((SHOTS, 1))
    shot_pixel = set_ends(jax.random.randint(key_of[6], (SHOTS,), 0, TILE * TILE), jax.random.fold_in(key_of[6], 1), 0, (TILE * TILE) - 1).astype(jnp.int32)
    shot_height = normal_values(key_of[7], (SHOTS,), 0.3, 2.0, ((0, 32),), jnp.float32)
    return dict(heights=heights, shadow=shadow, image_tiles=image_tiles, image_dest=image_dest, sun_gain=sun_gain, shot_dest=shot_dest, shot_pixel=shot_pixel, shot_height=shot_height)


sharpness = 8.0
step_size = 0.01
smooth_weight = 2.0
laser_weight = 20.0

def to_tiles(field):
    return field.reshape(N_ROW, TILE, N_COL, TILE).transpose(0, 2, 1, 3).reshape(N_ROW * N_COL, TILE, TILE)

def from_tiles(stacked):
    return stacked.reshape(N_ROW, N_COL, TILE, TILE).transpose(0, 2, 1, 3).reshape(N_ROW * TILE, N_COL * TILE)

def surface_terms(padded, center):
    slope_x = (padded[1:-1, 2:] - padded[1:-1, :-2]) * 0.5
    slope_y = (padded[2:, 1:-1] - padded[:-2, 1:-1]) * 0.5
    laplace = padded[2:, 1:-1] + padded[:-2, 1:-1] + padded[1:-1, 2:] + padded[1:-1, :-2] - 4.0 * center
    return (slope_x, slope_y, laplace)

def image_terms(slope_x, slope_y, pieces, angles):
    sun_x = angles[:, 0, None, None]
    sun_y = angles[:, 1, None, None]
    sun_z = angles[:, 2, None, None]
    gain = angles[:, 3, None, None]
    inverse = lax.rsqrt(1.0 + slope_x * slope_x + slope_y * slope_y)
    cosine = (sun_z - slope_x * sun_x - slope_y * sun_y) * inverse
    refl = jax.nn.softplus(sharpness * cosine) / sharpness
    sigma = jax.nn.sigmoid(sharpness * cosine)
    along_x = -sun_x * inverse - cosine * slope_x * inverse * inverse
    along_y = -sun_y * inverse - cosine * slope_y * inverse * inverse
    observed = pieces.astype(jnp.float32)
    seen = gain * observed * sigma
    model = gain * gain * refl * sigma
    return (seen * along_x, seen * along_y, model * along_x, model * along_y, gain * observed * refl, gain * gain * refl * refl)

def reference(heights, shadow, image_tiles, image_dest, sun_gain, shot_dest, shot_pixel, shot_height):
    lit = 1.0 - shadow.astype(jnp.float32)
    block = 128 if IMAGES % 128 == 0 else IMAGES
    groups = IMAGES // block
    pixels = image_tiles.reshape(groups, block, TILE, TILE)
    geometry = sun_gain.astype(jnp.float32).reshape(groups, block, 4)
    owners = image_dest[:, 0].astype(jnp.int32).reshape(groups, block)
    shot_owner = shot_dest[:, 0].astype(jnp.int32)
    grid_row = shot_owner // N_COL * TILE + shot_pixel // TILE
    grid_col = shot_owner % N_COL * TILE + shot_pixel % TILE
    flat_index = (grid_row * NW + grid_col).astype(jnp.int32)
    hits = jnp.zeros((NH * NW,), jnp.float32).at[flat_index].add(jnp.ones_like(shot_height)).reshape(NH, NW)
    height_sum = jnp.zeros((NH * NW,), jnp.float32).at[flat_index].add(shot_height).reshape(NH, NW)
    surface = heights
    for sweep in range(ITERS):
        padded = jnp.pad(surface, 1)
        slope_x, slope_y, laplace = surface_terms(padded, surface)
        tiles_x = to_tiles(slope_x)
        tiles_y = to_tiles(slope_y)

        def accumulate(carry, group):
            pieces, angles, owner_ids = group
            terms = image_terms(tiles_x[owner_ids], tiles_y[owner_ids], pieces, angles)
            return (tuple((total.at[owner_ids].add(term) for total, term in zip(carry, terms))), None)
        start = tuple((jnp.zeros((DEVICES, TILE, TILE), jnp.float32) for member in range(6)))
        totals, unused = lax.scan(accumulate, start, (pixels, geometry, owners))
        obs_x, obs_y, fit_x, fit_y, cross, power = [from_tiles(total) for total in totals]
        albedo = jnp.sum(lit * cross) / jnp.sum(lit * power)
        grad_x = lit * (albedo * albedo * fit_x - albedo * obs_x)
        grad_y = lit * (albedo * albedo * fit_y - albedo * obs_y)
        pad_x = jnp.pad(grad_x, 1)
        pad_y = jnp.pad(grad_y, 1)
        data = (pad_x[1:-1, :-2] - pad_x[1:-1, 2:]) * 0.5 + (pad_y[:-2, 1:-1] - pad_y[2:, 1:-1]) * 0.5
        surface = surface - step_size * (data - smooth_weight * laplace + laser_weight * (hits * surface - height_sum))
    return surface
```

```python
import functools
import math

import jax
import jax.numpy as jnp
from jax import lax
from jax.experimental import pallas as pl
from jax.experimental.pallas import tpu as pltpu
from jax.sharding import PartitionSpec as P

ITERS = 2

sharpness = 8.0
step_size = 0.01
smooth_weight = 2.0
laser_weight = 20.0

AXES = ("row", "col")
LOG2E = math.log2(math.e)
CHUNK = 16
LINK = jnp.float32


def rim_specs(side, cols, tiles, tile_of):
    def at(offset, block, where):
        def index(*args):
            tile = jnp.clip(tile_of(*args) + offset, 0, tiles - 1)
            return (tile,) + where

        return pl.BlockSpec((1,) + block, index)

    return [
        at(0, (side, side), (0, 0)),
        at(-cols, (8, side), (side // 8 - 1, 0)),
        at(cols, (8, side), (0, 0)),
        at(-1, (side, 128), (0, side // 128 - 1)),
        at(1, (side, 128), (0, 0)),
    ]


def edges(tile, rows, cols):
    row, col = tile // cols, lax.rem(tile, cols)
    as_gate = lambda test: jnp.where(test, 1.0, 0.0).astype(jnp.float32)
    return as_gate(row > 0), as_gate(row < rows - 1), as_gate(col > 0), as_gate(col < cols - 1)


def shifted(center, up, down, left, right):
    side = center.shape[0]
    row = lax.broadcasted_iota(jnp.int32, center.shape, 0)
    col = lax.broadcasted_iota(jnp.int32, center.shape, 1)
    above = jnp.where(row == 0, up, pltpu.roll(center, 1, 0))
    below = jnp.where(row == side - 1, down, pltpu.roll(center, side - 1, 0))
    before = jnp.where(col == 0, left, pltpu.roll(center, 1, 1))
    after = jnp.where(col == side - 1, right, pltpu.roll(center, side - 1, 1))
    return above, below, before, after


def image_kernel(
    rows, cols, order, tile, slot, first, last, sun,
    pixels, center, up, down, left, right, lit,
    obs_x, obs_y, fit_x, fit_y, cross, power,
    inv_s, px_s, py_s, ox_s, oy_s, fx_s, fy_s,
):
    i = pl.program_id(0)
    side = center.shape[1]

    @pl.when(i == 0)
    def start_sums():
        cross[...] = jnp.zeros_like(cross)
        power[...] = jnp.zeros_like(power)

    @pl.when(first[i] == 1)
    def start_tile():
        g_up, g_down, g_left, g_right = edges(tile[i], rows, cols)
        above, below, before, after = shifted(
            center[0],
            up[0, 7:8, :] * g_up,
            down[0, 0:1, :] * g_down,
            left[0, :, 127:128] * g_left,
            right[0, :, 0:1] * g_right,
        )
        slope_x = (after - before) * 0.5
        slope_y = (below - above) * 0.5
        inverse = lax.rsqrt(1.0 + slope_x * slope_x + slope_y * slope_y)
        inv_s[...] = inverse
        px_s[...] = slope_x * inverse
        py_s[...] = slope_y * inverse
        zero = jnp.zeros((side, side), jnp.float32)
        ox_s[...] = zero
        oy_s[...] = zero
        fx_s[...] = zero
        fy_s[...] = zero

    k = order[i]
    sx, sy, sz, gain = sun[4 * k], sun[4 * k + 1], sun[4 * k + 2], sun[4 * k + 3]
    scale = sharpness * LOG2E
    ux, uy, uz = sx * scale, sy * scale, sz * scale
    refl_scale = gain * (1.0 / (sharpness * LOG2E))
    gx, gy = gain * sx, gain * sy
    gc = gain * (1.0 / scale)

    def step(j, sums):
        at = pl.ds(pl.multiple_of(j * CHUNK, CHUNK), CHUNK)
        inverse, px, py = inv_s[at, :], px_s[at, :], py_s[at, :]
        observed = pixels[0, at, :].astype(jnp.float32)
        shine = lit[0, at, :].astype(jnp.float32)
        u = uz * inverse - ux * px - uy * py
        soft = jnp.log2(1.0 + jnp.exp2(u))
        sigma = 1.0 - jnp.exp2(-soft)
        q = soft * refl_scale
        v = u * gc
        dx = gx + v * px
        dy = gy + v * py
        seen = sigma * observed
        model = sigma * q
        ox_s[at, :] += seen * dx
        oy_s[at, :] += seen * dy
        fx_s[at, :] += model * dx
        fy_s[at, :] += model * dy
        shone = shine * q
        return sums[0] + shone * observed, sums[1] + shone * q

    zero = jnp.zeros((CHUNK, side), jnp.float32)
    sums = lax.fori_loop(0, side // CHUNK, step, (zero, zero), unroll=2)
    cross[...] += sums[0]
    power[...] += sums[1]

    @pl.when(last[i] == 1)
    def end_tile():
        factor = inv_s[...] * (-lit[0].astype(jnp.float32))
        obs_x[0] = (ox_s[...] * factor).astype(obs_x.dtype)
        obs_y[0] = (oy_s[...] * factor).astype(obs_y.dtype)
        fit_x[0] = (fx_s[...] * factor).astype(fit_x.dtype)
        fit_y[0] = (fy_s[...] * factor).astype(fit_y.dtype)


def image_sums(rows, cols, plan, sun, pixels, surface_all, lit_all):
    order, tile, slot, first, last = plan
    images, side = pixels.shape[0], pixels.shape[1]
    tiles = rows * cols
    slots = min(tiles, images)
    by_tile = lambda i, order, tile, *rest: tile[i]
    field = jax.ShapeDtypeStruct((slots, side, side), jnp.float32)
    part = jax.ShapeDtypeStruct((CHUNK, side), jnp.float32)
    field_spec = pl.BlockSpec((1, side, side), lambda i, order, tile, slot, *rest: (slot[i], 0, 0))
    part_spec = pl.BlockSpec((CHUNK, side), lambda i, *rest: (0, 0))
    return pl.pallas_call(
        functools.partial(image_kernel, rows, cols),
        out_shape=[field] * 4 + [part] * 2,
        grid_spec=pltpu.PrefetchScalarGridSpec(
            num_scalar_prefetch=6,
            grid=(images,),
            in_specs=[pl.BlockSpec((1, side, side), lambda i, order, *rest: (order[i], 0, 0))]
            + rim_specs(side, cols, tiles, by_tile)
            + [pl.BlockSpec((1, side, side), lambda i, order, tile, *rest: (tile[i], 0, 0))],
            out_specs=[field_spec] * 4 + [part_spec] * 2,
            scratch_shapes=[pltpu.VMEM((side, side), jnp.float32)] * 7,
        ),
        compiler_params=pltpu.CompilerParams(vmem_limit_bytes=40 * 2**20),
        name="image_sums",
    )(order, tile, slot, first, last, sun, pixels, *([surface_all] * 5), lit_all)


def data_kernel(
    rows, cols, slot, seen, albedo,
    ox, ox_l, ox_r, fx, fx_l, fx_r, oy, oy_u, oy_d, fy, fy_u, fy_d, out,
):
    t = pl.program_id(0)
    tiles = rows * cols
    g_up, g_down, g_left, g_right = edges(t, rows, cols)
    a = albedo[0]
    has = lambda n: jnp.where(seen[jnp.clip(n, 0, tiles - 1)] == 1, a, 0.0)
    here, above, below = has(t), has(t - cols) * g_up, has(t + cols) * g_down
    before, after = has(t - 1) * g_left, has(t + 1) * g_right
    mix = lambda f, o, gate: (a * f - o) * gate
    grad_x = mix(fx[0], ox[0], here)
    grad_y = mix(fy[0], oy[0], here)
    side = grad_x.shape[0]
    left = mix(fx_l[0, :, 127:128], ox_l[0, :, 127:128], before)
    right = mix(fx_r[0, :, 0:1], ox_r[0, :, 0:1], after)
    up = mix(fy_u[0, 7:8, :], oy_u[0, 7:8, :], above)
    down = mix(fy_d[0, 0:1, :], oy_d[0, 0:1, :], below)
    row = lax.broadcasted_iota(jnp.int32, grad_x.shape, 0)
    col = lax.broadcasted_iota(jnp.int32, grad_x.shape, 1)
    y_above = jnp.where(row == 0, up, pltpu.roll(grad_y, 1, 0))
    y_below = jnp.where(row == side - 1, down, pltpu.roll(grad_y, side - 1, 0))
    x_before = jnp.where(col == 0, left, pltpu.roll(grad_x, 1, 1))
    x_after = jnp.where(col == side - 1, right, pltpu.roll(grad_x, side - 1, 1))
    out[0] = ((x_before - x_after) * 0.5 + (y_above - y_below) * 0.5).astype(out.dtype)


def data_part(rows, cols, slot, seen, albedo, obs_x, obs_y, fit_x, fit_y):
    side = obs_x.shape[1]
    tiles = rows * cols
    center, up, down, left, right = rim_specs(side, cols, tiles, lambda t, *rest: t)

    def through(spec):
        def index(t, slot, *rest):
            place = spec.index_map(t)
            return (slot[place[0]],) + place[1:]

        return pl.BlockSpec(spec.block_shape, index)

    center, up, down, left, right = map(through, (center, up, down, left, right))
    return pl.pallas_call(
        functools.partial(data_kernel, rows, cols),
        out_shape=jax.ShapeDtypeStruct((tiles, side, side), jnp.float32),
        grid_spec=pltpu.PrefetchScalarGridSpec(
            num_scalar_prefetch=3,
            grid=(tiles,),
            in_specs=[center, left, right] * 2 + [center, up, down] * 2,
            out_specs=pl.BlockSpec((1, side, side), lambda t, *rest: (t, 0, 0)),
        ),
        compiler_params=pltpu.CompilerParams(vmem_limit_bytes=40 * 2**20),
        name="data_part",
    )(
        slot, seen, albedo,
        obs_x, obs_x, obs_x, fit_x, fit_x, fit_x, obs_y, obs_y, obs_y, fit_y, fit_y, fit_y,
    )


def update_kernel(rows, cols, me, center, up, down, left, right, data, out):
    g_up, g_down, g_left, g_right = edges(me[0], rows, cols)
    surface = center[0]
    above, below, before, after = shifted(
        surface,
        up[0, 7:8, :] * g_up,
        down[0, 0:1, :] * g_down,
        left[0, :, 127:128] * g_left,
        right[0, :, 0:1] * g_right,
    )
    laplace = below + above + after + before - 4.0 * surface
    out[...] = surface - step_size * (data[...].astype(jnp.float32) - smooth_weight * laplace)


def update(rows, cols, me, surface_all, data):
    side = data.shape[0]
    whole = pl.BlockSpec((side, side), lambda i, me: (0, 0))
    return pl.pallas_call(
        functools.partial(update_kernel, rows, cols),
        out_shape=jax.ShapeDtypeStruct((side, side), jnp.float32),
        grid_spec=pltpu.PrefetchScalarGridSpec(
            num_scalar_prefetch=1,
            grid=(1,),
            in_specs=rim_specs(side, cols, rows * cols, lambda i, me: me[0]) + [whole],
            out_specs=whole,
        ),
        compiler_params=pltpu.CompilerParams(vmem_limit_bytes=40 * 2**20),
        name="update",
    )(me, *([surface_all] * 5), data)


def total_kernel(rows, cols, part, total, held, send_sem, recv_sem):
    devices = rows * cols
    me = lax.axis_index("row") * cols + lax.axis_index("col")
    barrier = pltpu.get_barrier_semaphore()

    def place(step):
        peer = lax.rem(me + step, devices)
        return peer, (peer // cols, lax.rem(peer, cols))

    def greet(step, carry):
        unused, device = place(step)
        pl.semaphore_signal(barrier, inc=1, device_id=device, device_id_type=pl.DeviceIdType.MESH)
        return carry

    lax.fori_loop(1, devices, greet, 0)
    pl.semaphore_wait(barrier, devices - 1)

    def copy(step):
        unused, device = place(step)
        return pltpu.make_async_remote_copy(
            src_ref=part,
            dst_ref=held.at[step],
            send_sem=send_sem.at[step],
            recv_sem=recv_sem.at[step],
            device_id=device,
            device_id_type=pl.DeviceIdType.MESH,
        )

    def send(step, carry):
        copy(step).start()
        return carry

    def land(step, carry):
        copy(step).wait()
        return carry

    held[0] = part[...]
    lax.fori_loop(1, devices, send, 0)
    lax.fori_loop(1, devices, land, 0)
    total[...] = jnp.sum(held[...], axis=0)


def total_over_devices(rows, cols, part):
    devices = rows * cols
    return pl.pallas_call(
        functools.partial(total_kernel, rows, cols),
        out_shape=jax.ShapeDtypeStruct(part.shape, jnp.float32),
        in_specs=[pl.BlockSpec(memory_space=pltpu.VMEM)],
        out_specs=pl.BlockSpec(memory_space=pltpu.VMEM),
        scratch_shapes=[
            pltpu.VMEM((devices,) + part.shape, jnp.float32),
            pltpu.SemaphoreType.DMA((devices,)),
            pltpu.SemaphoreType.DMA((devices,)),
        ],
        compiler_params=pltpu.CompilerParams(collective_id=0, has_side_effects=True),
        name="total",
    )(part)


def image_plan(dest, tiles):
    count = dest.shape[0]
    place = jnp.arange(count)
    earlier = (dest[None, :] < dest[:, None]) | (
        (dest[None, :] == dest[:, None]) & (place[None, :] < place[:, None])
    )
    rank = jnp.sum(earlier, axis=1)
    chosen = rank[None, :] == place[:, None]
    order = jnp.sum(jnp.where(chosen, place[None, :], 0), axis=1).astype(jnp.int32)
    tile = jnp.sum(jnp.where(chosen, dest[None, :], 0), axis=1).astype(jnp.int32)
    seen = jnp.any(dest[None, :] == jnp.arange(tiles)[:, None], axis=1)
    before = jnp.arange(tiles)[None, :] < jnp.arange(tiles)[:, None]
    tile_slot = jnp.where(seen, jnp.sum(before & seen[None, :], axis=1), 0).astype(jnp.int32)
    slot = jnp.sum(
        jnp.where(tile[:, None] == jnp.arange(tiles)[None, :], tile_slot[None, :], 0), axis=1
    ).astype(jnp.int32)
    change = (tile[1:] != tile[:-1]).astype(jnp.int32)
    one = jnp.ones((1,), jnp.int32)
    first = jnp.concatenate([one, change])
    last = jnp.concatenate([change, one])
    return (order, tile, slot, first, last), tile_slot, seen.astype(jnp.int32)


def body(heights, shadow, image_tiles, image_dest, sun_gain, shot_dest, shot_pixel, shot_height):
    rows, cols = lax.axis_size("row"), lax.axis_size("col")
    tiles = rows * cols
    side = heights.shape[0]
    me = (lax.axis_index("row") * cols + lax.axis_index("col")).astype(jnp.int32).reshape(1)
    plan, tile_slot, seen = image_plan(image_dest[:, 0], tiles)
    sun = sun_gain.astype(jnp.float32).reshape(-1)
    lit_all = lax.all_gather((1.0 - shadow.astype(jnp.float32)).astype(jnp.bfloat16), AXES)
    shot_at = (shot_dest[:, 0], shot_pixel // side, lax.rem(shot_pixel, side))
    surface = heights
    for sweep in range(ITERS):
        surface_all = lax.all_gather(surface, AXES)
        obs_x, obs_y, fit_x, fit_y, cross, power = image_sums(
            rows, cols, plan, sun, image_tiles, surface_all, lit_all
        )
        sums = jnp.stack([jnp.sum(cross), jnp.sum(power)])
        sums = jnp.broadcast_to(sums[:, None, None], (2, 4, 128)).reshape(8, 128)
        sums = total_over_devices(rows, cols, sums)
        albedo = (sums[0, 0] / sums[4, 0]).reshape(1)
        data = data_part(rows, cols, tile_slot, seen, albedo, obs_x, obs_y, fit_x, fit_y)
        misfit = laser_weight * (surface_all[shot_at] - shot_height)
        data = data.at[shot_at].add(misfit)
        data = lax.psum_scatter(data.astype(LINK), AXES, scatter_dimension=0, tiled=False)
        surface = update(rows, cols, me, surface_all, data)
    return surface


def solution(mesh):
    placed = (
        P("row", "col"),
        P("row", "col"),
        P(("row", "col"), None, None),
        P(("row", "col"), None),
        P(("row", "col"), None),
        P(("row", "col"), None),
        P(("row", "col")),
        P(("row", "col")),
    )
    return jax.shard_map(
        body, mesh=mesh, in_specs=placed, out_specs=P("row", "col"), check_vma=False
    )
```

```python
import functools
import math

import jax
import jax.numpy as jnp
from jax import lax
from jax.experimental import pallas as pl
from jax.experimental.pallas import tpu as pltpu
from jax.sharding import PartitionSpec as P

ITERS = 2

sharpness = 8.0
step_size = 0.01
smooth_weight = 2.0
laser_weight = 20.0

AXES = ("row", "col")
LOG2E = math.log2(math.e)
CHUNK = 16
LINK = jnp.bfloat16


def rim_specs(side, cols, tiles, tile_of):
    def at(offset, block, where):
        def index(*args):
            tile = jnp.clip(tile_of(*args) + offset, 0, tiles - 1)
            return (tile,) + where

        return pl.BlockSpec((1,) + block, index)

    return [
        at(0, (side, side), (0, 0)),
        at(-cols, (8, side), (side // 8 - 1, 0)),
        at(cols, (8, side), (0, 0)),
        at(-1, (side, 128), (0, side // 128 - 1)),
        at(1, (side, 128), (0, 0)),
    ]


def edges(tile, rows, cols):
    row, col = tile // cols, lax.rem(tile, cols)
    as_gate = lambda test: jnp.where(test, 1.0, 0.0).astype(jnp.float32)
    return as_gate(row > 0), as_gate(row < rows - 1), as_gate(col > 0), as_gate(col < cols - 1)


def shifted(center, up, down, left, right):
    side = center.shape[0]
    row = lax.broadcasted_iota(jnp.int32, center.shape, 0)
    col = lax.broadcasted_iota(jnp.int32, center.shape, 1)
    above = jnp.where(row == 0, up, pltpu.roll(center, 1, 0))
    below = jnp.where(row == side - 1, down, pltpu.roll(center, side - 1, 0))
    before = jnp.where(col == 0, left, pltpu.roll(center, 1, 1))
    after = jnp.where(col == side - 1, right, pltpu.roll(center, side - 1, 1))
    return above, below, before, after


def image_kernel(
    rows, cols, order, tile, slot, first, last, sun,
    pixels, center, up, down, left, right, lit,
    obs_x, obs_y, fit_x, fit_y, cross, power,
    inv_s, px_s, py_s, ox_s, oy_s, fx_s, fy_s,
):
    i = pl.program_id(0)
    side = center.shape[1]

    @pl.when(i == 0)
    def start_sums():
        cross[...] = jnp.zeros_like(cross)
        power[...] = jnp.zeros_like(power)

    @pl.when(first[i] == 1)
    def start_tile():
        g_up, g_down, g_left, g_right = edges(tile[i], rows, cols)
        above, below, before, after = shifted(
            center[0],
            up[0, 7:8, :] * g_up,
            down[0, 0:1, :] * g_down,
            left[0, :, 127:128] * g_left,
            right[0, :, 0:1] * g_right,
        )
        slope_x = (after - before) * 0.5
        slope_y = (below - above) * 0.5
        inverse = lax.rsqrt(1.0 + slope_x * slope_x + slope_y * slope_y)
        inv_s[...] = inverse
        px_s[...] = slope_x * inverse
        py_s[...] = slope_y * inverse
        zero = jnp.zeros((side, side), jnp.float32)
        ox_s[...] = zero
        oy_s[...] = zero
        fx_s[...] = zero
        fy_s[...] = zero

    k = order[i]
    sx, sy, sz, gain = sun[4 * k], sun[4 * k + 1], sun[4 * k + 2], sun[4 * k + 3]
    scale = sharpness * LOG2E
    ux, uy, uz = sx * scale, sy * scale, sz * scale
    refl_scale = gain * (1.0 / (sharpness * LOG2E))
    gx, gy = gain * sx, gain * sy
    gc = gain * (1.0 / scale)

    def step(j, sums):
        at = pl.ds(pl.multiple_of(j * CHUNK, CHUNK), CHUNK)
        inverse, px, py = inv_s[at, :], px_s[at, :], py_s[at, :]
        observed = pixels[0, at, :].astype(jnp.float32)
        shine = lit[0, at, :].astype(jnp.float32)
        u = uz * inverse - ux * px - uy * py
        soft = jnp.log2(1.0 + jnp.exp2(u))
        sigma = 1.0 - jnp.exp2(-soft)
        q = soft * refl_scale
        v = u * gc
        dx = gx + v * px
        dy = gy + v * py
        seen = sigma * observed
        model = sigma * q
        ox_s[at, :] += seen * dx
        oy_s[at, :] += seen * dy
        fx_s[at, :] += model * dx
        fy_s[at, :] += model * dy
        shone = shine * q
        return sums[0] + shone * observed, sums[1] + shone * q

    zero = jnp.zeros((CHUNK, side), jnp.float32)
    sums = lax.fori_loop(0, side // CHUNK, step, (zero, zero), unroll=2)
    cross[...] += sums[0]
    power[...] += sums[1]

    @pl.when(last[i] == 1)
    def end_tile():
        factor = inv_s[...] * (-lit[0].astype(jnp.float32))
        obs_x[0] = (ox_s[...] * factor).astype(obs_x.dtype)
        obs_y[0] = (oy_s[...] * factor).astype(obs_y.dtype)
        fit_x[0] = (fx_s[...] * factor).astype(fit_x.dtype)
        fit_y[0] = (fy_s[...] * factor).astype(fit_y.dtype)


def image_sums(rows, cols, plan, sun, pixels, surface_all, lit_all):
    order, tile, slot, first, last = plan
    images, side = pixels.shape[0], pixels.shape[1]
    tiles = rows * cols
    slots = min(tiles, images)
    by_tile = lambda i, order, tile, *rest: tile[i]
    field = jax.ShapeDtypeStruct((slots, side, side), jnp.float32)
    part = jax.ShapeDtypeStruct((CHUNK, side), jnp.float32)
    field_spec = pl.BlockSpec((1, side, side), lambda i, order, tile, slot, *rest: (slot[i], 0, 0))
    part_spec = pl.BlockSpec((CHUNK, side), lambda i, *rest: (0, 0))
    return pl.pallas_call(
        functools.partial(image_kernel, rows, cols),
        out_shape=[field] * 4 + [part] * 2,
        grid_spec=pltpu.PrefetchScalarGridSpec(
            num_scalar_prefetch=6,
            grid=(images,),
            in_specs=[pl.BlockSpec((1, side, side), lambda i, order, *rest: (order[i], 0, 0))]
            + rim_specs(side, cols, tiles, by_tile)
            + [pl.BlockSpec((1, side, side), lambda i, order, tile, *rest: (tile[i], 0, 0))],
            out_specs=[field_spec] * 4 + [part_spec] * 2,
            scratch_shapes=[pltpu.VMEM((side, side), jnp.float32)] * 7,
        ),
        compiler_params=pltpu.CompilerParams(vmem_limit_bytes=40 * 2**20),
        name="image_sums",
    )(order, tile, slot, first, last, sun, pixels, *([surface_all] * 5), lit_all)


def data_kernel(
    rows, cols, slot, seen, albedo, shot_start, shot_pixel, shot_height,
    ox, ox_l, ox_r, fx, fx_l, fx_r, oy, oy_u, oy_d, fy, fy_u, fy_d, surface, out,
):
    t = pl.program_id(0)
    tiles = rows * cols
    g_up, g_down, g_left, g_right = edges(t, rows, cols)
    a = albedo[0]
    has = lambda n: jnp.where(seen[jnp.clip(n, 0, tiles - 1)] == 1, a, 0.0)
    here, above, below = has(t), has(t - cols) * g_up, has(t + cols) * g_down
    before, after = has(t - 1) * g_left, has(t + 1) * g_right
    mix = lambda f, o, gate: (a * f - o) * gate
    grad_x = mix(fx[0], ox[0], here)
    grad_y = mix(fy[0], oy[0], here)
    side = grad_x.shape[0]
    left = mix(fx_l[0, :, 127:128], ox_l[0, :, 127:128], before)
    right = mix(fx_r[0, :, 0:1], ox_r[0, :, 0:1], after)
    up = mix(fy_u[0, 7:8, :], oy_u[0, 7:8, :], above)
    down = mix(fy_d[0, 0:1, :], oy_d[0, 0:1, :], below)
    row = lax.broadcasted_iota(jnp.int32, grad_x.shape, 0)
    col = lax.broadcasted_iota(jnp.int32, grad_x.shape, 1)
    y_above = jnp.where(row == 0, up, pltpu.roll(grad_y, 1, 0))
    y_below = jnp.where(row == side - 1, down, pltpu.roll(grad_y, side - 1, 0))
    x_before = jnp.where(col == 0, left, pltpu.roll(grad_x, 1, 1))
    x_after = jnp.where(col == side - 1, right, pltpu.roll(grad_x, side - 1, 1))
    out[0] = (x_before - x_after) * 0.5 + (y_above - y_below) * 0.5
    lane = lax.broadcasted_iota(jnp.int32, (1, side), 1)

    def shot(n, carry):
        pixel = shot_pixel[n]
        at = pl.ds(pixel // side, 1)
        misfit = laser_weight * (surface[0, at, :] - shot_height[n])
        out[0, at, :] += jnp.where(lane == lax.rem(pixel, side), misfit, 0.0)
        return carry

    lax.fori_loop(shot_start[t], shot_start[t + 1], shot, 0)


def data_part(rows, cols, slot, seen, albedo, shots, surface_all, obs_x, obs_y, fit_x, fit_y):
    side = obs_x.shape[1]
    tiles = rows * cols
    center, up, down, left, right = rim_specs(side, cols, tiles, lambda t, *rest: t)

    def through(spec):
        def index(t, slot, *rest):
            place = spec.index_map(t)
            return (slot[place[0]],) + place[1:]

        return pl.BlockSpec(spec.block_shape, index)

    center, up, down, left, right = map(through, (center, up, down, left, right))
    return pl.pallas_call(
        functools.partial(data_kernel, rows, cols),
        out_shape=jax.ShapeDtypeStruct((tiles, side, side), jnp.float32),
        grid_spec=pltpu.PrefetchScalarGridSpec(
            num_scalar_prefetch=6,
            grid=(tiles,),
            in_specs=[center, left, right] * 2
            + [center, up, down] * 2
            + [pl.BlockSpec((1, side, side), lambda t, *rest: (t, 0, 0))],
            out_specs=pl.BlockSpec((1, side, side), lambda t, *rest: (t, 0, 0)),
        ),
        compiler_params=pltpu.CompilerParams(vmem_limit_bytes=40 * 2**20),
        name="data_part",
    )(
        slot, seen, albedo, *shots,
        obs_x, obs_x, obs_x, fit_x, fit_x, fit_x, obs_y, obs_y, obs_y, fit_y, fit_y, fit_y,
        surface_all,
    )


def update_kernel(rows, cols, me, center, up, down, left, right, data, out):
    g_up, g_down, g_left, g_right = edges(me[0], rows, cols)
    surface = center[0]
    above, below, before, after = shifted(
        surface,
        up[0, 7:8, :] * g_up,
        down[0, 0:1, :] * g_down,
        left[0, :, 127:128] * g_left,
        right[0, :, 0:1] * g_right,
    )
    laplace = below + above + after + before - 4.0 * surface
    out[...] = surface - step_size * (data[...].astype(jnp.float32) - smooth_weight * laplace)


def update(rows, cols, me, surface_all, data):
    side = data.shape[0]
    whole = pl.BlockSpec((side, side), lambda i, me: (0, 0))
    return pl.pallas_call(
        functools.partial(update_kernel, rows, cols),
        out_shape=jax.ShapeDtypeStruct((side, side), jnp.float32),
        grid_spec=pltpu.PrefetchScalarGridSpec(
            num_scalar_prefetch=1,
            grid=(1,),
            in_specs=rim_specs(side, cols, rows * cols, lambda i, me: me[0]) + [whole],
            out_specs=whole,
        ),
        compiler_params=pltpu.CompilerParams(vmem_limit_bytes=40 * 2**20),
        name="update",
    )(me, *([surface_all] * 5), data)


def total_kernel(rows, cols, part, total, held, send_sem, recv_sem):
    devices = rows * cols
    me = lax.axis_index("row") * cols + lax.axis_index("col")
    barrier = pltpu.get_barrier_semaphore()

    def place(step):
        peer = lax.rem(me + step, devices)
        return peer, (peer // cols, lax.rem(peer, cols))

    def greet(step, carry):
        unused, device = place(step)
        pl.semaphore_signal(barrier, inc=1, device_id=device, device_id_type=pl.DeviceIdType.MESH)
        return carry

    lax.fori_loop(1, devices, greet, 0)
    pl.semaphore_wait(barrier, devices - 1)

    def copy(step):
        unused, device = place(step)
        return pltpu.make_async_remote_copy(
            src_ref=part,
            dst_ref=held.at[step],
            send_sem=send_sem.at[step],
            recv_sem=recv_sem.at[step],
            device_id=device,
            device_id_type=pl.DeviceIdType.MESH,
        )

    def send(step, carry):
        copy(step).start()
        return carry

    def land(step, carry):
        copy(step).wait()
        return carry

    held[0] = part[...]
    lax.fori_loop(1, devices, send, 0)
    lax.fori_loop(1, devices, land, 0)
    total[...] = jnp.sum(held[...], axis=0)


def total_over_devices(rows, cols, part):
    devices = rows * cols
    return pl.pallas_call(
        functools.partial(total_kernel, rows, cols),
        out_shape=jax.ShapeDtypeStruct(part.shape, jnp.float32),
        in_specs=[pl.BlockSpec(memory_space=pltpu.VMEM)],
        out_specs=pl.BlockSpec(memory_space=pltpu.VMEM),
        scratch_shapes=[
            pltpu.VMEM((devices,) + part.shape, jnp.float32),
            pltpu.SemaphoreType.DMA((devices,)),
            pltpu.SemaphoreType.DMA((devices,)),
        ],
        compiler_params=pltpu.CompilerParams(collective_id=0, has_side_effects=True),
        name="total",
    )(part)


def add_kernel(
    rows, cols, data, out,
    own, got1, send2, got2, send3, got3, send4, got4,
    load_sem, ss1, rs1, ss2, rs2, ss3, rs3, ss4, rs4,
):
    X, Z = rows // 2, cols // 2
    side = out.shape[0]
    r, c = lax.axis_index("row"), lax.axis_index("col")
    x, k, z, y = r // 2, lax.rem(r, 2), c // 2, lax.rem(c, 2)
    core_peer = (x * 2 + 1 - k, c)
    y_peer = (r, z * 2 + 1 - y)
    x_at = [lax.rem(x + d, X) for d in range(X)]
    z_at = [lax.rem(z + e + 1, Z) for e in range(Z)]
    x_peers = [None] + [(x_at[d] * 2 + k, c) for d in range(1, X)]
    z_peers = [(r, z_at[e] * 2 + y) for e in range(Z - 1)]

    barrier = pltpu.get_barrier_semaphore()
    peers = [core_peer, y_peer] + x_peers[1:] + z_peers
    for peer in peers:
        pl.semaphore_signal(barrier, inc=1, device_id=peer, device_id_type=pl.DeviceIdType.MESH)
    pl.semaphore_wait(barrier, len(peers))

    def remote(src, dst, send, recv, peer):
        return pltpu.make_async_remote_copy(
            src_ref=src, dst_ref=dst, send_sem=send, recv_sem=recv,
            device_id=peer, device_id_type=pl.DeviceIdType.MESH,
        )

    first = [
        remote(data.at[:, 1 - k, z_at[e]], got1.at[e], ss1.at[e], rs1.at[e], core_peer)
        for e in range(Z)
    ]
    loads = [
        pltpu.make_async_copy(data.at[:, k, z_at[e]], own.at[e], load_sem.at[e]) for e in range(Z)
    ]
    second = [
        [
            remote(send2.at[e, d - 1], got2.at[e, d - 1], ss2.at[e, d - 1], rs2.at[e, d - 1], x_peers[d])
            for d in range(1, X)
        ]
        for e in range(Z)
    ]
    third = [remote(send3.at[e], got3.at[e], ss3.at[e], rs3.at[e], y_peer) for e in range(Z)]
    fourth = [
        remote(send4.at[e], got4.at[e], ss4.at[e], rs4.at[e], z_peers[e]) for e in range(Z - 1)
    ]
    for e in range(Z):
        first[e].start()
        loads[e].start()

    def by_rows(work):
        def step(j, carry):
            work(pl.ds(pl.multiple_of(j * 32, 32), 32))
            return carry

        lax.fori_loop(0, side // 32, step, 0)

    def over_x(e, which, at):
        total = own[e, x, which, at, :] + got1[e, x, which, at, :]
        for d in range(1, X):
            total = total + got2[e, d - 1, which, at, :].astype(jnp.float32)
        return total

    def stage2(e):
        loads[e].wait()
        first[e].wait_recv()
        for d in range(1, X):

            def work(at):
                for which in range(2):
                    total = own[e, x_at[d], which, at, :] + got1[e, x_at[d], which, at, :]
                    send2[e, d - 1, which, at, :] = total.astype(LINK)

            by_rows(work)
            second[e][d - 1].start()

    def stage3(e):
        for copy in second[e]:
            copy.wait_recv()

        def work(at):
            send3[e, at, :] = over_x(e, 1 - y, at).astype(LINK)

        by_rows(work)
        third[e].start()

    def stage4(e):
        third[e].wait_recv()

        def work(at):
            total = over_x(e, y, at) + got3[e, at, :].astype(jnp.float32)
            if e < Z - 1:
                send4[e, at, :] = total.astype(LINK)
            else:
                out[at, :] = total

        by_rows(work)
        if e < Z - 1:
            fourth[e].start()

    for t in range(Z + 2):
        if t < Z:
            stage2(t)
        if 0 <= t - 1 < Z:
            stage3(t - 1)
        if 0 <= t - 2 < Z:
            stage4(t - 2)
    for copy in fourth:
        copy.wait_recv()

    def finish(at):
        total = out[at, :]
        for e in range(Z - 1):
            total = total + got4[e, at, :].astype(jnp.float32)
        out[at, :] = total

    by_rows(finish)
    for copy in first + [one for some in second for one in some] + third + fourth:
        copy.wait_send()


def add_parts(rows, cols, data):
    X, Z = rows // 2, cols // 2
    side = data.shape[-1]
    vmem = lambda shape, dtype: pltpu.VMEM(shape + (side, side), dtype)
    dma = pltpu.SemaphoreType.DMA
    return pl.pallas_call(
        functools.partial(add_kernel, rows, cols),
        out_shape=jax.ShapeDtypeStruct((side, side), jnp.float32),
        in_specs=[pl.BlockSpec(memory_space=pl.ANY)],
        out_specs=pl.BlockSpec(memory_space=pltpu.VMEM),
        scratch_shapes=[
            vmem((Z, X, 2), jnp.float32),
            vmem((Z, X, 2), jnp.float32),
            vmem((Z, X - 1, 2), LINK),
            vmem((Z, X - 1, 2), LINK),
            vmem((Z,), LINK),
            vmem((Z,), LINK),
            vmem((Z - 1,), LINK),
            vmem((Z - 1,), LINK),
            dma((Z,)),
            dma((Z,)),
            dma((Z,)),
            dma((Z, X - 1)),
            dma((Z, X - 1)),
            dma((Z,)),
            dma((Z,)),
            dma((Z - 1,)),
            dma((Z - 1,)),
        ],
        compiler_params=pltpu.CompilerParams(
            collective_id=1, has_side_effects=True, vmem_limit_bytes=56 * 2**20
        ),
        name="add_parts",
    )(data.reshape(X, 2, Z, 2, side, side))


def image_plan(dest, tiles):
    count = dest.shape[0]
    place = jnp.arange(count)
    earlier = (dest[None, :] < dest[:, None]) | (
        (dest[None, :] == dest[:, None]) & (place[None, :] < place[:, None])
    )
    rank = jnp.sum(earlier, axis=1)
    chosen = rank[None, :] == place[:, None]
    order = jnp.sum(jnp.where(chosen, place[None, :], 0), axis=1).astype(jnp.int32)
    tile = jnp.sum(jnp.where(chosen, dest[None, :], 0), axis=1).astype(jnp.int32)
    seen = jnp.any(dest[None, :] == jnp.arange(tiles)[:, None], axis=1)
    before = jnp.arange(tiles)[None, :] < jnp.arange(tiles)[:, None]
    tile_slot = jnp.where(seen, jnp.sum(before & seen[None, :], axis=1), 0).astype(jnp.int32)
    slot = jnp.sum(
        jnp.where(tile[:, None] == jnp.arange(tiles)[None, :], tile_slot[None, :], 0), axis=1
    ).astype(jnp.int32)
    change = (tile[1:] != tile[:-1]).astype(jnp.int32)
    one = jnp.ones((1,), jnp.int32)
    first = jnp.concatenate([one, change])
    last = jnp.concatenate([change, one])
    return (order, tile, slot, first, last), tile_slot, seen.astype(jnp.int32)


def shot_plan(dest, pixel, height, tiles):
    place = jnp.arange(dest.shape[0])
    earlier = (dest[None, :] < dest[:, None]) | (
        (dest[None, :] == dest[:, None]) & (place[None, :] < place[:, None])
    )
    rank = jnp.sum(earlier, axis=1)
    chosen = rank[None, :] == place[:, None]
    pixel = jnp.sum(jnp.where(chosen, pixel[None, :], 0), axis=1).astype(jnp.int32)
    height = jnp.sum(jnp.where(chosen, height[None, :], 0.0), axis=1)
    start = jnp.sum(dest[None, :] < jnp.arange(tiles + 1)[:, None], axis=1).astype(jnp.int32)
    return start, pixel, height


def body(heights, shadow, image_tiles, image_dest, sun_gain, shot_dest, shot_pixel, shot_height):
    rows, cols = lax.axis_size("row"), lax.axis_size("col")
    tiles = rows * cols
    side = heights.shape[0]
    me = (lax.axis_index("row") * cols + lax.axis_index("col")).astype(jnp.int32).reshape(1)
    plan, tile_slot, seen = image_plan(image_dest[:, 0], tiles)
    sun = sun_gain.astype(jnp.float32).reshape(-1)
    lit_all = lax.all_gather((1.0 - shadow.astype(jnp.float32)).astype(jnp.bfloat16), AXES)
    shots = shot_plan(shot_dest[:, 0], shot_pixel, shot_height, tiles)
    surface = heights
    for sweep in range(ITERS):
        surface_all = lax.all_gather(surface, AXES)
        obs_x, obs_y, fit_x, fit_y, cross, power = image_sums(
            rows, cols, plan, sun, image_tiles, surface_all, lit_all
        )
        sums = jnp.stack([jnp.sum(cross), jnp.sum(power)])
        sums = jnp.broadcast_to(sums[:, None, None], (2, 4, 128)).reshape(8, 128)
        sums = total_over_devices(rows, cols, sums)
        albedo = (sums[0, 0] / sums[4, 0]).reshape(1)
        data = data_part(
            rows, cols, tile_slot, seen, albedo, shots, surface_all, obs_x, obs_y, fit_x, fit_y
        )
        data = add_parts(rows, cols, data)
        surface = update(rows, cols, me, surface_all, data)
    return surface


def solution(mesh):
    placed = (
        P("row", "col"),
        P("row", "col"),
        P(("row", "col"), None, None),
        P(("row", "col"), None),
        P(("row", "col"), None),
        P(("row", "col"), None),
        P(("row", "col")),
        P(("row", "col")),
    )
    return jax.shard_map(
        body, mesh=mesh, in_specs=placed, out_specs=P("row", "col"), check_vma=False
    )
```

```python
import functools
import math

import jax
import jax.numpy as jnp
from jax import lax
from jax.experimental import pallas as pl
from jax.experimental.pallas import tpu as pltpu
from jax.sharding import PartitionSpec as P

ITERS = 2

sharpness = 8.0
step_size = 0.01
smooth_weight = 2.0
laser_weight = 20.0

AXES = ("row", "col")
LOG2E = math.log2(math.e)
CHUNK = 16
LINK = jnp.bfloat16
VMEM_BYTES = 60 * 2**20


def rim_specs(side, cols, tiles, tile_of, high=8):
    def at(offset, block, where):
        def index(*args):
            tile = jnp.clip(tile_of(*args) + offset, 0, tiles - 1)
            return (tile,) + where

        return pl.BlockSpec((1,) + block, index)

    return [
        at(0, (side, side), (0, 0)),
        at(-cols, (high, side), (side // high - 1, 0)),
        at(cols, (high, side), (0, 0)),
        at(-1, (side, 128), (0, side // 128 - 1)),
        at(1, (side, 128), (0, 0)),
    ]


def edges(tile, rows, cols):
    row, col = tile // cols, lax.rem(tile, cols)
    as_gate = lambda test: jnp.where(test, 1.0, 0.0).astype(jnp.float32)
    return as_gate(row > 0), as_gate(row < rows - 1), as_gate(col > 0), as_gate(col < cols - 1)


def shifted(center, up, down, left, right):
    side = center.shape[0]
    row = lax.broadcasted_iota(jnp.int32, center.shape, 0)
    col = lax.broadcasted_iota(jnp.int32, center.shape, 1)
    above = jnp.where(row == 0, up, pltpu.roll(center, 1, 0))
    below = jnp.where(row == side - 1, down, pltpu.roll(center, side - 1, 0))
    before = jnp.where(col == 0, left, pltpu.roll(center, 1, 1))
    after = jnp.where(col == side - 1, right, pltpu.roll(center, side - 1, 1))
    return above, below, before, after


def image_kernel(
    rows, cols, order, tile, start, sun,
    pixels, center, up, down, left, right, lit,
    obs_x, obs_y, fit_x, fit_y, part,
    inv_s, px_s, py_s, ox_s, oy_s, fx_s, fy_s, cross, power,
):
    i = pl.program_id(0)
    side = center.shape[1]

    @pl.when(i == 0)
    def start_sums():
        cross[...] = jnp.zeros_like(cross)
        power[...] = jnp.zeros_like(power)

    @pl.when(start[i + 1] > start[i])
    def start_tile():
        g_up, g_down, g_left, g_right = edges(tile[i], rows, cols)
        above, below, before, after = shifted(
            center[0],
            up[0, 7:8, :] * g_up,
            down[0, 0:1, :] * g_down,
            left[0, :, 127:128] * g_left,
            right[0, :, 0:1] * g_right,
        )
        slope_x = (after - before) * 0.5
        slope_y = (below - above) * 0.5
        inverse = lax.rsqrt(1.0 + slope_x * slope_x + slope_y * slope_y)
        inv_s[...] = inverse
        px_s[...] = slope_x * inverse
        py_s[...] = slope_y * inverse

    def step(fresh, numbers, j, sums):
        k, ux, uy, uz, refl_scale, gx, gy, gc = numbers
        at = pl.ds(pl.multiple_of(j * CHUNK, CHUNK), CHUNK)
        inverse, px, py = inv_s[at, :], px_s[at, :], py_s[at, :]
        observed = pixels[k, at, :].astype(jnp.float32)
        shine = lit[0, at, :].astype(jnp.float32)
        u = uz * inverse - ux * px - uy * py
        soft = jnp.log2(1.0 + jnp.exp2(u))
        sigma = 1.0 - jnp.exp2(-soft)
        q = soft * refl_scale
        v = u * gc
        dx = gx + v * px
        dy = gy + v * py
        seen = sigma * observed
        model = sigma * q
        for held, term in (
            (ox_s, seen * dx), (oy_s, seen * dy), (fx_s, model * dx), (fy_s, model * dy)
        ):
            held[at, :] = term if fresh else held[at, :] + term
        shone = shine * q
        return sums[0] + shone * observed, sums[1] + shone * q

    def sweep(fresh, n):
        k = order[n]
        sx, sy, sz, gain = sun[4 * k], sun[4 * k + 1], sun[4 * k + 2], sun[4 * k + 3]
        scale = sharpness * LOG2E
        numbers = (
            k, sx * scale, sy * scale, sz * scale,
            gain * (1.0 / scale), gain * sx, gain * sy, gain * (1.0 / scale),
        )
        zero = jnp.zeros((CHUNK, side), jnp.float32)
        sums = lax.fori_loop(
            0, side // CHUNK, functools.partial(step, fresh, numbers), (zero, zero), unroll=2
        )
        cross[...] += sums[0]
        power[...] += sums[1]

    def more(n, carry):
        sweep(False, n)
        return carry

    pl.when(start[i + 1] > start[i])(lambda: sweep(True, start[i]))
    lax.fori_loop(start[i] + 1, start[i + 1], more, 0)

    @pl.when(start[i + 1] > start[i])
    def end_tile():
        factor = inv_s[...] * (-lit[0].astype(jnp.float32))
        obs_x[0] = (ox_s[...] * factor).astype(obs_x.dtype)
        obs_y[0] = (oy_s[...] * factor).astype(obs_y.dtype)
        fit_x[0] = (fx_s[...] * factor).astype(fit_x.dtype)
        fit_y[0] = (fy_s[...] * factor).astype(fit_y.dtype)

    @pl.when(i == pl.num_programs(0) - 1)
    def end_sums():
        for n, held in enumerate((cross, power)):
            total = jnp.zeros((8, 128), jnp.float32)
            for a in range(CHUNK // 8):
                for b in range(side // 128):
                    total = total + held[8 * a : 8 * a + 8, 128 * b : 128 * b + 128]
            part[8 * n : 8 * n + 8, :] = total


def image_sums(rows, cols, plan, sun, pixels, surface_all, lit_all):
    order, tile, start = plan
    images, side = pixels.shape[0], pixels.shape[1]
    tiles = rows * cols
    slots = min(tiles, images)
    by_tile = lambda i, order, tile, *rest: tile[i]
    field = jax.ShapeDtypeStruct((slots, side, side), jnp.bfloat16)
    part = jax.ShapeDtypeStruct((16, 128), jnp.float32)
    field_spec = pl.BlockSpec((1, side, side), lambda i, *rest: (i, 0, 0))
    part_spec = pl.BlockSpec((16, 128), lambda i, *rest: (0, 0))
    return pl.pallas_call(
        functools.partial(image_kernel, rows, cols),
        out_shape=[field] * 4 + [part],
        grid_spec=pltpu.PrefetchScalarGridSpec(
            num_scalar_prefetch=4,
            grid=(slots,),
            in_specs=[pl.BlockSpec(memory_space=pltpu.VMEM)]
            + rim_specs(side, cols, tiles, by_tile)
            + [pl.BlockSpec((1, side, side), lambda i, order, tile, *rest: (tile[i], 0, 0))],
            out_specs=[field_spec] * 4 + [part_spec],
            scratch_shapes=[pltpu.VMEM((side, side), jnp.float32)] * 7
            + [pltpu.VMEM((CHUNK, side), jnp.float32)] * 2,
        ),
        compiler_params=pltpu.CompilerParams(vmem_limit_bytes=VMEM_BYTES),
        name="image_sums",
    )(order, tile, start, sun, pixels, *([surface_all] * 5), lit_all)


def data_kernel(
    rows, cols, slot, seen, albedo, shot_start, shot_pixel, shot_height,
    ox, ox_l, ox_r, fx, fx_l, fx_r, oy, oy_u, oy_d, fy, fy_u, fy_d, surface, out,
):
    t = pl.program_id(0)
    tiles = rows * cols
    g_up, g_down, g_left, g_right = edges(t, rows, cols)
    a = albedo[0]
    has = lambda n: jnp.where(seen[jnp.clip(n, 0, tiles - 1)] == 1, a, 0.0)
    here, above, below = has(t), has(t - cols) * g_up, has(t + cols) * g_down
    before, after = has(t - 1) * g_left, has(t + 1) * g_right
    mix = lambda f, o, gate: (a * f.astype(jnp.float32) - o.astype(jnp.float32)) * gate
    grad_x = mix(fx[0], ox[0], here)
    grad_y = mix(fy[0], oy[0], here)
    side = grad_x.shape[0]
    left = mix(fx_l[0], ox_l[0], before)[:, 127:128]
    right = mix(fx_r[0], ox_r[0], after)[:, 0:1]
    up = mix(fy_u[0], oy_u[0], above)[15:16, :]
    down = mix(fy_d[0], oy_d[0], below)[0:1, :]
    row = lax.broadcasted_iota(jnp.int32, grad_x.shape, 0)
    col = lax.broadcasted_iota(jnp.int32, grad_x.shape, 1)
    y_above = jnp.where(row == 0, up, pltpu.roll(grad_y, 1, 0))
    y_below = jnp.where(row == side - 1, down, pltpu.roll(grad_y, side - 1, 0))
    x_before = jnp.where(col == 0, left, pltpu.roll(grad_x, 1, 1))
    x_after = jnp.where(col == side - 1, right, pltpu.roll(grad_x, side - 1, 1))
    out[0] = (x_before - x_after) * 0.5 + (y_above - y_below) * 0.5
    lane = lax.broadcasted_iota(jnp.int32, (1, side), 1)

    def shot(n, carry):
        pixel = shot_pixel[n]
        at = pl.ds(pixel // side, 1)
        misfit = laser_weight * (surface[0, at, :] - shot_height[n])
        out[0, at, :] += jnp.where(lane == lax.rem(pixel, side), misfit, 0.0)
        return carry

    lax.fori_loop(shot_start[t], shot_start[t + 1], shot, 0)


def data_part(rows, cols, slot, seen, albedo, shots, surface_all, obs_x, obs_y, fit_x, fit_y):
    side = obs_x.shape[1]
    tiles = rows * cols
    center, up, down, left, right = rim_specs(side, cols, tiles, lambda t, *rest: t, 16)

    def through(spec):
        def index(t, slot, *rest):
            place = spec.index_map(t)
            return (slot[place[0]],) + place[1:]

        return pl.BlockSpec(spec.block_shape, index)

    center, up, down, left, right = map(through, (center, up, down, left, right))
    return pl.pallas_call(
        functools.partial(data_kernel, rows, cols),
        out_shape=jax.ShapeDtypeStruct((tiles, side, side), jnp.float32),
        grid_spec=pltpu.PrefetchScalarGridSpec(
            num_scalar_prefetch=6,
            grid=(tiles,),
            in_specs=[center, left, right] * 2
            + [center, up, down] * 2
            + [pl.BlockSpec((1, side, side), lambda t, *rest: (t, 0, 0))],
            out_specs=pl.BlockSpec((1, side, side), lambda t, *rest: (t, 0, 0)),
        ),
        compiler_params=pltpu.CompilerParams(vmem_limit_bytes=VMEM_BYTES),
        name="data_part",
    )(
        slot, seen, albedo, *shots,
        obs_x, obs_x, obs_x, fit_x, fit_x, fit_x, obs_y, obs_y, obs_y, fit_y, fit_y, fit_y,
        surface_all,
    )


def update_kernel(rows, cols, me, center, up, down, left, right, data, out):
    g_up, g_down, g_left, g_right = edges(me[0], rows, cols)
    surface = center[0]
    above, below, before, after = shifted(
        surface,
        up[0, 7:8, :] * g_up,
        down[0, 0:1, :] * g_down,
        left[0, :, 127:128] * g_left,
        right[0, :, 0:1] * g_right,
    )
    laplace = below + above + after + before - 4.0 * surface
    out[...] = surface - step_size * (data[...].astype(jnp.float32) - smooth_weight * laplace)


def update(rows, cols, me, surface_all, data):
    side = data.shape[0]
    whole = pl.BlockSpec((side, side), lambda i, me: (0, 0))
    return pl.pallas_call(
        functools.partial(update_kernel, rows, cols),
        out_shape=jax.ShapeDtypeStruct((side, side), jnp.float32),
        grid_spec=pltpu.PrefetchScalarGridSpec(
            num_scalar_prefetch=1,
            grid=(1,),
            in_specs=rim_specs(side, cols, rows * cols, lambda i, me: me[0]) + [whole],
            out_specs=whole,
        ),
        compiler_params=pltpu.CompilerParams(vmem_limit_bytes=VMEM_BYTES),
        name="update",
    )(me, *([surface_all] * 5), data)


def total_kernel(rows, cols, part, total, held, send_sem, recv_sem):
    devices = rows * cols
    me = lax.axis_index("row") * cols + lax.axis_index("col")
    barrier = pltpu.get_barrier_semaphore()

    def place(step):
        peer = lax.rem(me + step, devices)
        return peer, (peer // cols, lax.rem(peer, cols))

    def greet(step, carry):
        unused, device = place(step)
        pl.semaphore_signal(barrier, inc=1, device_id=device, device_id_type=pl.DeviceIdType.MESH)
        return carry

    lax.fori_loop(1, devices, greet, 0)
    pl.semaphore_wait(barrier, devices - 1)

    def copy(step):
        unused, device = place(step)
        return pltpu.make_async_remote_copy(
            src_ref=part,
            dst_ref=held.at[step],
            send_sem=send_sem.at[step],
            recv_sem=recv_sem.at[step],
            device_id=device,
            device_id_type=pl.DeviceIdType.MESH,
        )

    def send(step, carry):
        copy(step).start()
        return carry

    def land(step, carry):
        copy(step).wait()
        return carry

    held[0] = part[...]
    lax.fori_loop(1, devices, send, 0)
    lax.fori_loop(1, devices, land, 0)
    sums = jnp.sum(held[...], axis=0)
    total[...] = jnp.full(total.shape, jnp.sum(sums[:8]) / jnp.sum(sums[8:]), jnp.float32)


def total_over_devices(rows, cols, part):
    devices = rows * cols
    return pl.pallas_call(
        functools.partial(total_kernel, rows, cols),
        out_shape=jax.ShapeDtypeStruct((8, 128), jnp.float32),
        in_specs=[pl.BlockSpec(memory_space=pltpu.VMEM)],
        out_specs=pl.BlockSpec(memory_space=pltpu.VMEM),
        scratch_shapes=[
            pltpu.VMEM((devices,) + part.shape, jnp.float32),
            pltpu.SemaphoreType.DMA((devices,)),
            pltpu.SemaphoreType.DMA((devices,)),
        ],
        compiler_params=pltpu.CompilerParams(
            collective_id=0, has_side_effects=True, vmem_limit_bytes=VMEM_BYTES
        ),
        name="total",
    )(part)


def add_kernel(
    rows, cols, data, out,
    own, got1, send2, got2, send3, got3, send4, got4,
    load_sem, ss1, rs1, ss2, rs2, ss3, rs3, ss4, rs4,
):
    X, Z = rows // 2, cols // 2
    side = out.shape[0]
    r, c = lax.axis_index("row"), lax.axis_index("col")
    x, k, z, y = r // 2, lax.rem(r, 2), c // 2, lax.rem(c, 2)
    core_peer = (x * 2 + 1 - k, c)
    y_peer = (r, z * 2 + 1 - y)
    x_at = [lax.rem(x + d, X) for d in range(X)]
    z_at = [lax.rem(z + e + 1, Z) for e in range(Z)]
    x_peers = [None] + [(x_at[d] * 2 + k, c) for d in range(1, X)]
    z_peers = [(r, z_at[e] * 2 + y) for e in range(Z - 1)]

    barrier = pltpu.get_barrier_semaphore()
    peers = [core_peer, y_peer] + x_peers[1:] + z_peers
    for peer in peers:
        pl.semaphore_signal(barrier, inc=1, device_id=peer, device_id_type=pl.DeviceIdType.MESH)
    pl.semaphore_wait(barrier, len(peers))

    def remote(src, dst, send, recv, peer):
        return pltpu.make_async_remote_copy(
            src_ref=src, dst_ref=dst, send_sem=send, recv_sem=recv,
            device_id=peer, device_id_type=pl.DeviceIdType.MESH,
        )

    first = [
        remote(data.at[:, 1 - k, z_at[e]], got1.at[e], ss1.at[e], rs1.at[e], core_peer)
        for e in range(Z)
    ]
    loads = [
        pltpu.make_async_copy(data.at[:, k, z_at[e]], own.at[e], load_sem.at[e]) for e in range(Z)
    ]
    second = [
        [
            remote(send2.at[e, d - 1], got2.at[e, d - 1], ss2.at[e, d - 1], rs2.at[e, d - 1], x_peers[d])
            for d in range(1, X)
        ]
        for e in range(Z)
    ]
    third = [remote(send3.at[e], got3.at[e], ss3.at[e], rs3.at[e], y_peer) for e in range(Z)]
    fourth = [
        remote(send4.at[e], got4.at[e], ss4.at[e], rs4.at[e], z_peers[e]) for e in range(Z - 1)
    ]
    for e in range(Z):
        first[e].start()
        loads[e].start()

    def by_rows(work):
        def step(j, carry):
            work(pl.ds(pl.multiple_of(j * 32, 32), 32))
            return carry

        lax.fori_loop(0, side // 32, step, 0)

    def over_x(e, which, at):
        total = own[e, x, which, at, :] + got1[e, x, which, at, :]
        for d in range(1, X):
            total = total + got2[e, d - 1, which, at, :].astype(jnp.float32)
        return total

    def stage2(e):
        loads[e].wait()
        first[e].wait_recv()
        for d in range(1, X):

            def work(at):
                for which in range(2):
                    total = own[e, x_at[d], which, at, :] + got1[e, x_at[d], which, at, :]
                    send2[e, d - 1, which, at, :] = total.astype(LINK)

            by_rows(work)
            second[e][d - 1].start()

    def stage3(e):
        for copy in second[e]:
            copy.wait_recv()

        def work(at):
            send3[e, at, :] = over_x(e, 1 - y, at).astype(LINK)

        by_rows(work)
        third[e].start()

    def stage4(e):
        third[e].wait_recv()

        def work(at):
            total = over_x(e, y, at) + got3[e, at, :].astype(jnp.float32)
            if e < Z - 1:
                send4[e, at, :] = total.astype(LINK)
            else:
                out[at, :] = total

        by_rows(work)
        if e < Z - 1:
            fourth[e].start()

    for t in range(Z + 2):
        if t < Z:
            stage2(t)
        if 0 <= t - 1 < Z:
            stage3(t - 1)
        if 0 <= t - 2 < Z:
            stage4(t - 2)
    for copy in fourth:
        copy.wait_recv()

    def finish(at):
        total = out[at, :]
        for e in range(Z - 1):
            total = total + got4[e, at, :].astype(jnp.float32)
        out[at, :] = total

    by_rows(finish)
    for copy in first + [one for some in second for one in some] + third + fourth:
        copy.wait_send()


def add_parts(rows, cols, data):
    X, Z = rows // 2, cols // 2
    side = data.shape[-1]
    vmem = lambda shape, dtype: pltpu.VMEM(shape + (side, side), dtype)
    dma = pltpu.SemaphoreType.DMA
    return pl.pallas_call(
        functools.partial(add_kernel, rows, cols),
        out_shape=jax.ShapeDtypeStruct((side, side), jnp.float32),
        in_specs=[pl.BlockSpec(memory_space=pl.ANY)],
        out_specs=pl.BlockSpec(memory_space=pltpu.VMEM),
        scratch_shapes=[
            vmem((Z, X, 2), jnp.float32),
            vmem((Z, X, 2), jnp.float32),
            vmem((Z, X - 1, 2), LINK),
            vmem((Z, X - 1, 2), LINK),
            vmem((Z,), LINK),
            vmem((Z,), LINK),
            vmem((Z - 1,), LINK),
            vmem((Z - 1,), LINK),
            dma((Z,)),
            dma((Z,)),
            dma((Z,)),
            dma((Z, X - 1)),
            dma((Z, X - 1)),
            dma((Z,)),
            dma((Z,)),
            dma((Z - 1,)),
            dma((Z - 1,)),
        ],
        compiler_params=pltpu.CompilerParams(
            collective_id=1, has_side_effects=True, vmem_limit_bytes=VMEM_BYTES
        ),
        name="add_parts",
    )(data.reshape(X, 2, Z, 2, side, side))


def gather_kernel(rows, cols, count, *refs):
    mine, outs = refs[:count], refs[count : 2 * count]
    local_sem, sz, rz, sa, ra, sb, rb, sc, rc = refs[2 * count :]
    X, Z = rows // 2, cols // 2
    side = mine[0].shape[0]
    half = side // 2
    r, c = lax.axis_index("row"), lax.axis_index("col")
    x, k, z, y = r // 2, lax.rem(r, 2), c // 2, lax.rem(c, 2)
    core_peer = (x * 2 + 1 - k, c)
    x_peers = [(lax.rem(x + d, X) * 2 + k, c) for d in range(1, X)]
    y_peers = [(r, z * 2 + 1 - y)]
    z_peers = [(r, lax.rem(z + d, Z) * 2 + y) for d in range(1, Z)]
    source = [lax.rem(z + Z - d, Z) for d in range(Z)]

    barrier = pltpu.get_barrier_semaphore()
    peers = [core_peer] + x_peers + y_peers + z_peers
    for peer in peers:
        pl.semaphore_signal(barrier, inc=1, device_id=peer, device_id_type=pl.DeviceIdType.MESH)
    pl.semaphore_wait(barrier, len(peers))

    def remote(src, dst, send, recv, peer):
        return pltpu.make_async_remote_copy(
            src_ref=src, dst_ref=dst, send_sem=send, recv_sem=recv,
            device_id=peer, device_id_type=pl.DeviceIdType.MESH,
        )

    own = [pltpu.make_async_copy(mine[n], outs[n].at[x, k, z, y], local_sem.at[n]) for n in range(count)]
    streams = []
    for n in range(count):
        own[n].start()
        for h in range(2):
            part = pl.ds(h * half, half)
            s = 2 * n + h
            along_z = [
                remote(
                    mine[n].at[part], outs[n].at[x, k, z, y, part],
                    sz.at[s, d], rz.at[s, d], z_peers[d],
                )
                for d in range(Z - 1)
            ]
            a_peers, b_peers = (x_peers, y_peers) if h else (y_peers, x_peers)
            along_a, along_b, along_core = [], [], []
            for e in range(Z):
                tile = outs[n].at[x, k, source[e], y, part]
                slab = outs[n].at[:, k, source[e], y, part] if h else outs[n].at[x, k, source[e], :, part]
                full = outs[n].at[:, k, source[e], :, part]
                along_a.append(
                    [
                        remote(tile, tile, sa.at[s, e, d], ra.at[s, e, d], peer)
                        for d, peer in enumerate(a_peers)
                    ]
                )
                along_b.append(
                    [
                        remote(slab, slab, sb.at[s, e, d], rb.at[s, e, d], peer)
                        for d, peer in enumerate(b_peers)
                    ]
                )
                along_core.append(remote(full, full, sc.at[s, e], rc.at[s, e], core_peer))
            for copy in along_z:
                copy.start()
            streams.append((along_z, along_a, along_b, along_core))
    for copy in own:
        copy.wait()
    for t in range(Z + 2):
        for along_z, along_a, along_b, along_core in streams:
            if t < Z:
                if t:
                    along_z[t - 1].wait_recv()
                for copy in along_a[t]:
                    copy.start()
            if 0 <= t - 1 < Z:
                for copy in along_a[t - 1]:
                    copy.wait_recv()
                for copy in along_b[t - 1]:
                    copy.start()
            if 0 <= t - 2 < Z:
                for copy in along_b[t - 2]:
                    copy.wait_recv()
                along_core[t - 2].start()
    for along_z, along_a, along_b, along_core in streams:
        for copy in along_core:
            copy.wait_recv()
        for copy in along_z + sum(along_a, []) + sum(along_b, []) + along_core:
            copy.wait_send()


def gather(rows, cols, values, collective):
    X, Z = rows // 2, cols // 2
    count, most = len(values), max(X - 1, 1)
    side = values[0].shape[0]
    anywhere = pl.BlockSpec(memory_space=pl.ANY)
    dma = pltpu.SemaphoreType.DMA
    streams = 2 * count
    outs = pl.pallas_call(
        functools.partial(gather_kernel, rows, cols, count),
        out_shape=[jax.ShapeDtypeStruct((X, 2, Z, 2, side, side), v.dtype) for v in values],
        in_specs=[anywhere] * count,
        out_specs=[anywhere] * count,
        scratch_shapes=[dma((count,))]
        + [dma((streams, Z - 1))] * 2
        + [dma((streams, Z, most))] * 4
        + [dma((streams, Z))] * 2,
        compiler_params=pltpu.CompilerParams(
            collective_id=collective, has_side_effects=True, vmem_limit_bytes=VMEM_BYTES
        ),
        name="gather",
    )(*values)
    return [out.reshape(rows * cols, side, side) for out in outs]


def image_plan(dest, tiles):
    count = dest.shape[0]
    place = jnp.arange(count)
    earlier = (dest[None, :] < dest[:, None]) | (
        (dest[None, :] == dest[:, None]) & (place[None, :] < place[:, None])
    )
    rank = jnp.sum(earlier, axis=1)
    chosen = rank[None, :] == place[:, None]
    order = jnp.sum(jnp.where(chosen, place[None, :], 0), axis=1).astype(jnp.int32)
    seen = jnp.any(dest[None, :] == jnp.arange(tiles)[:, None], axis=1)
    before = jnp.arange(tiles)[None, :] < jnp.arange(tiles)[:, None]
    tile_slot = jnp.where(seen, jnp.sum(before & seen[None, :], axis=1), 0).astype(jnp.int32)
    slots = jnp.arange(min(tiles, count) + 1)
    held = seen[None, :] & (tile_slot[None, :] == slots[:-1, None])
    slot_tile = jnp.sum(jnp.where(held, jnp.arange(tiles)[None, :], 0), axis=1).astype(jnp.int32)
    named = jnp.sum(dest[None, :] == jnp.arange(tiles)[:, None], axis=1)
    past = seen[None, :] & (tile_slot[None, :] < slots[:, None])
    start = jnp.sum(jnp.where(past, named[None, :], 0), axis=1).astype(jnp.int32)
    return (order, slot_tile, start), tile_slot, seen.astype(jnp.int32)


def shot_plan(dest, pixel, height, tiles):
    place = jnp.arange(dest.shape[0])
    earlier = (dest[None, :] < dest[:, None]) | (
        (dest[None, :] == dest[:, None]) & (place[None, :] < place[:, None])
    )
    rank = jnp.sum(earlier, axis=1)
    chosen = rank[None, :] == place[:, None]
    pixel = jnp.sum(jnp.where(chosen, pixel[None, :], 0), axis=1).astype(jnp.int32)
    height = jnp.sum(jnp.where(chosen, height[None, :], 0.0), axis=1)
    start = jnp.sum(dest[None, :] < jnp.arange(tiles + 1)[:, None], axis=1).astype(jnp.int32)
    return start, pixel, height


def body(heights, shadow, image_tiles, image_dest, sun_gain, shot_dest, shot_pixel, shot_height):
    rows, cols = lax.axis_size("row"), lax.axis_size("col")
    tiles = rows * cols
    side = heights.shape[0]
    me = (lax.axis_index("row") * cols + lax.axis_index("col")).astype(jnp.int32).reshape(1)
    plan, tile_slot, seen = image_plan(image_dest[:, 0], tiles)
    sun = sun_gain.astype(jnp.float32).reshape(-1)
    lit = (1 - shadow).astype(jnp.bfloat16)
    shots = shot_plan(shot_dest[:, 0], shot_pixel, shot_height, tiles)
    surface = heights
    for sweep in range(ITERS):
        if sweep == 0:
            surface_all, lit_all = gather(rows, cols, [surface, lit], 2)
        else:
            (surface_all,) = gather(rows, cols, [surface], 3)
        obs_x, obs_y, fit_x, fit_y, part = image_sums(
            rows, cols, plan, sun, image_tiles, surface_all, lit_all
        )
        albedo = total_over_devices(rows, cols, part)[0, :1]
        data = data_part(
            rows, cols, tile_slot, seen, albedo, shots, surface_all, obs_x, obs_y, fit_x, fit_y
        )
        data = add_parts(rows, cols, data)
        surface = update(rows, cols, me, surface_all, data)
    return surface


def solution(mesh):
    placed = (
        P("row", "col"),
        P("row", "col"),
        P(("row", "col"), None, None),
        P(("row", "col"), None),
        P(("row", "col"), None),
        P(("row", "col"), None),
        P(("row", "col")),
        P(("row", "col")),
    )
    return jax.shard_map(
        body, mesh=mesh, in_specs=placed, out_specs=P("row", "col"), check_vma=False
    )
```

```python
import functools
import math

import jax
import jax.numpy as jnp
from jax import lax
from jax.experimental import pallas as pl
from jax.experimental.pallas import tpu as pltpu
from jax.sharding import PartitionSpec as P

ITERS = 2

sharpness = 8.0
step_size = 0.01
smooth_weight = 2.0
laser_weight = 20.0

AXES = ("row", "col")
LOG2E = math.log2(math.e)
CHUNK = 16
LINK = jnp.bfloat16
VMEM_BYTES = 60 * 2**20


def rim_specs(side, cols, tiles, tile_of, high=8):
    def at(offset, block, where):
        def index(*args):
            tile = jnp.clip(tile_of(*args) + offset, 0, tiles - 1)
            return (tile,) + where

        return pl.BlockSpec((1,) + block, index)

    return [
        at(0, (side, side), (0, 0)),
        at(-cols, (high, side), (side // high - 1, 0)),
        at(cols, (high, side), (0, 0)),
        at(-1, (side, 128), (0, side // 128 - 1)),
        at(1, (side, 128), (0, 0)),
    ]


def edges(tile, rows, cols):
    row, col = tile // cols, lax.rem(tile, cols)
    as_gate = lambda test: jnp.where(test, 1.0, 0.0).astype(jnp.float32)
    return as_gate(row > 0), as_gate(row < rows - 1), as_gate(col > 0), as_gate(col < cols - 1)


def shifted(center, up, down, left, right):
    side = center.shape[0]
    row = lax.broadcasted_iota(jnp.int32, center.shape, 0)
    col = lax.broadcasted_iota(jnp.int32, center.shape, 1)
    above = jnp.where(row == 0, up, pltpu.roll(center, 1, 0))
    below = jnp.where(row == side - 1, down, pltpu.roll(center, side - 1, 0))
    before = jnp.where(col == 0, left, pltpu.roll(center, 1, 1))
    after = jnp.where(col == side - 1, right, pltpu.roll(center, side - 1, 1))
    return above, below, before, after


def image_kernel(
    rows, cols, order, tile, start, sun,
    pixels, center, up, down, left, right, lit,
    obs_x, obs_y, fit_x, fit_y, part,
    inv_s, px_s, py_s, ox_s, oy_s, fx_s, fy_s, cross, power,
):
    i = pl.program_id(0)
    side = center.shape[1]

    @pl.when(i == 0)
    def start_sums():
        cross[...] = jnp.zeros_like(cross)
        power[...] = jnp.zeros_like(power)

    @pl.when(start[i + 1] > start[i])
    def start_tile():
        g_up, g_down, g_left, g_right = edges(tile[i], rows, cols)
        row = lax.broadcasted_iota(jnp.int32, (CHUNK, side), 0)
        col = lax.broadcasted_iota(jnp.int32, (CHUNK, side), 1)
        top = up[0, 7:8, :] * g_up
        bottom = down[0, 0:1, :] * g_down
        chunks = side // CHUNK

        def slopes(j, carry):
            at = pl.ds(pl.multiple_of(j * CHUNK, CHUNK), CHUNK)
            here = center[0, at, :]
            higher = center[0, pl.ds(jnp.maximum(j * CHUNK - 1, 0), 1), :]
            lower = center[0, pl.ds(jnp.minimum(j * CHUNK + CHUNK, side - 1), 1), :]
            higher = jnp.where(j == 0, top, higher)
            lower = jnp.where(j == chunks - 1, bottom, lower)
            above = jnp.where(row == 0, higher, pltpu.roll(here, 1, 0))
            below = jnp.where(row == CHUNK - 1, lower, pltpu.roll(here, CHUNK - 1, 0))
            before = jnp.where(col == 0, left[0, at, 127:128] * g_left, pltpu.roll(here, 1, 1))
            after = jnp.where(
                col == side - 1, right[0, at, 0:1] * g_right, pltpu.roll(here, side - 1, 1)
            )
            slope_x = (after - before) * 0.5
            slope_y = (below - above) * 0.5
            inverse = lax.rsqrt(1.0 + slope_x * slope_x + slope_y * slope_y)
            inv_s[at, :] = inverse
            px_s[at, :] = slope_x * inverse
            py_s[at, :] = slope_y * inverse
            return carry

        lax.fori_loop(0, chunks, slopes, 0, unroll=2)

    def step(fresh, numbers, j, sums):
        k, ux, uy, uz, refl_scale, gx, gy, gc = numbers
        at = pl.ds(pl.multiple_of(j * CHUNK, CHUNK), CHUNK)
        inverse, px, py = inv_s[at, :], px_s[at, :], py_s[at, :]
        observed = pixels[k, at, :].astype(jnp.float32)
        shine = lit[0, at, :].astype(jnp.float32)
        u = uz * inverse - ux * px - uy * py
        soft = jnp.log2(1.0 + jnp.exp2(u))
        sigma = 1.0 - jnp.exp2(-soft)
        q = soft * refl_scale
        v = u * gc
        dx = gx + v * px
        dy = gy + v * py
        seen = sigma * observed
        model = sigma * q
        for held, term in (
            (ox_s, seen * dx), (oy_s, seen * dy), (fx_s, model * dx), (fy_s, model * dy)
        ):
            held[at, :] = term if fresh else held[at, :] + term
        shone = shine * q
        return sums[0] + shone * observed, sums[1] + shone * q

    def sweep(fresh, n):
        k = order[n]
        sx, sy, sz, gain = sun[4 * k], sun[4 * k + 1], sun[4 * k + 2], sun[4 * k + 3]
        scale = sharpness * LOG2E
        numbers = (
            k, sx * scale, sy * scale, sz * scale,
            gain * (1.0 / scale), gain * sx, gain * sy, gain * (1.0 / scale),
        )
        zero = jnp.zeros((CHUNK, side), jnp.float32)
        sums = lax.fori_loop(
            0, side // CHUNK, functools.partial(step, fresh, numbers), (zero, zero), unroll=2
        )
        cross[...] += sums[0]
        power[...] += sums[1]

    def more(n, carry):
        sweep(False, n)
        return carry

    pl.when(start[i + 1] > start[i])(lambda: sweep(True, start[i]))
    lax.fori_loop(start[i] + 1, start[i + 1], more, 0)

    @pl.when(start[i + 1] > start[i])
    def end_tile():
        def write(j, carry):
            at = pl.ds(pl.multiple_of(j * CHUNK, CHUNK), CHUNK)
            factor = inv_s[at, :] * (-lit[0, at, :].astype(jnp.float32))
            for field, held in ((obs_x, ox_s), (obs_y, oy_s), (fit_x, fx_s), (fit_y, fy_s)):
                field[0, at, :] = (held[at, :] * factor).astype(field.dtype)
            return carry

        lax.fori_loop(0, side // CHUNK, write, 0, unroll=2)

    @pl.when(i == pl.num_programs(0) - 1)
    def end_sums():
        for n, held in enumerate((cross, power)):
            total = jnp.zeros((8, 128), jnp.float32)
            for a in range(CHUNK // 8):
                for b in range(side // 128):
                    total = total + held[8 * a : 8 * a + 8, 128 * b : 128 * b + 128]
            part[8 * n : 8 * n + 8, :] = total


def image_sums(rows, cols, plan, sun, pixels, surface_all, lit_all):
    order, tile, start = plan
    images, side = pixels.shape[0], pixels.shape[1]
    tiles = rows * cols
    slots = min(tiles, images)
    by_tile = lambda i, order, tile, *rest: tile[i]
    field = jax.ShapeDtypeStruct((slots, side, side), jnp.bfloat16)
    part = jax.ShapeDtypeStruct((16, 128), jnp.float32)
    field_spec = pl.BlockSpec((1, side, side), lambda i, *rest: (i, 0, 0))
    part_spec = pl.BlockSpec((16, 128), lambda i, *rest: (0, 0))
    return pl.pallas_call(
        functools.partial(image_kernel, rows, cols),
        out_shape=[field] * 4 + [part],
        grid_spec=pltpu.PrefetchScalarGridSpec(
            num_scalar_prefetch=4,
            grid=(slots,),
            in_specs=[pl.BlockSpec(memory_space=pltpu.VMEM)]
            + rim_specs(side, cols, tiles, by_tile)
            + [pl.BlockSpec((1, side, side), lambda i, order, tile, *rest: (tile[i], 0, 0))],
            out_specs=[field_spec] * 4 + [part_spec],
            scratch_shapes=[pltpu.VMEM((side, side), jnp.float32)] * 7
            + [pltpu.VMEM((CHUNK, side), jnp.float32)] * 2,
        ),
        compiler_params=pltpu.CompilerParams(vmem_limit_bytes=VMEM_BYTES),
        name="image_sums",
    )(order, tile, start, sun, pixels, *([surface_all] * 5), lit_all)


def data_kernel(
    rows, cols, slot, seen, albedo, shot_start, shot_pixel, shot_height,
    ox, ox_l, ox_r, fx, fx_l, fx_r, oy, oy_u, oy_d, fy, fy_u, fy_d, surface, out,
):
    t = pl.program_id(0)
    tiles = rows * cols
    g_up, g_down, g_left, g_right = edges(t, rows, cols)
    a = albedo[0]
    has = lambda n: jnp.where(seen[jnp.clip(n, 0, tiles - 1)] == 1, a, 0.0)
    here, above, below = has(t), has(t - cols) * g_up, has(t + cols) * g_down
    before, after = has(t - 1) * g_left, has(t + 1) * g_right
    mix = lambda f, o, gate: (a * f.astype(jnp.float32) - o.astype(jnp.float32)) * gate
    side = out.shape[1]
    chunks = side // CHUNK
    row = lax.broadcasted_iota(jnp.int32, (CHUNK, side), 0)
    col = lax.broadcasted_iota(jnp.int32, (CHUNK, side), 1)
    rows_of = lambda j: pl.ds(pl.multiple_of(j * CHUNK, CHUNK), CHUNK)
    grad_y = lambda j: mix(fy[0, rows_of(j), :], oy[0, rows_of(j), :], here)
    top = mix(fy_u[0], oy_u[0], above)[15:16, :]
    bottom = mix(fy_d[0], oy_d[0], below)[0:1, :]

    def part(j, carry):
        higher, y = carry
        at = rows_of(j)
        x = mix(fx[0, at, :], ox[0, at, :], here)
        left = mix(fx_l[0, at, :], ox_l[0, at, :], before)[:, 127:128]
        right = mix(fx_r[0, at, :], ox_r[0, at, :], after)[:, 0:1]
        y_next = grad_y(jnp.minimum(j + 1, chunks - 1))
        lower = jnp.where(j == chunks - 1, bottom, y_next[0:1, :])
        y_above = jnp.where(row == 0, higher, pltpu.roll(y, 1, 0))
        y_below = jnp.where(row == CHUNK - 1, lower, pltpu.roll(y, CHUNK - 1, 0))
        x_before = jnp.where(col == 0, left, pltpu.roll(x, 1, 1))
        x_after = jnp.where(col == side - 1, right, pltpu.roll(x, side - 1, 1))
        out[0, at, :] = (x_before - x_after) * 0.5 + (y_above - y_below) * 0.5
        return y[CHUNK - 1 : CHUNK, :], y_next

    lax.fori_loop(0, chunks, part, (top, grad_y(0)), unroll=2)
    lane = lax.broadcasted_iota(jnp.int32, (1, side), 1)

    def shot(n, carry):
        pixel = shot_pixel[n]
        at = pl.ds(pixel // side, 1)
        misfit = laser_weight * (surface[0, at, :] - shot_height[n])
        out[0, at, :] += jnp.where(lane == lax.rem(pixel, side), misfit, 0.0)
        return carry

    lax.fori_loop(shot_start[t], shot_start[t + 1], shot, 0)


def data_part(rows, cols, slot, seen, albedo, shots, surface_all, obs_x, obs_y, fit_x, fit_y):
    side = obs_x.shape[1]
    tiles = rows * cols
    center, up, down, left, right = rim_specs(side, cols, tiles, lambda t, *rest: t, 16)

    def through(spec):
        def index(t, slot, *rest):
            place = spec.index_map(t)
            return (slot[place[0]],) + place[1:]

        return pl.BlockSpec(spec.block_shape, index)

    center, up, down, left, right = map(through, (center, up, down, left, right))
    return pl.pallas_call(
        functools.partial(data_kernel, rows, cols),
        out_shape=jax.ShapeDtypeStruct((tiles, side, side), jnp.float32),
        grid_spec=pltpu.PrefetchScalarGridSpec(
            num_scalar_prefetch=6,
            grid=(tiles,),
            in_specs=[center, left, right] * 2
            + [center, up, down] * 2
            + [pl.BlockSpec((1, side, side), lambda t, *rest: (t, 0, 0))],
            out_specs=pl.BlockSpec((1, side, side), lambda t, *rest: (t, 0, 0)),
        ),
        compiler_params=pltpu.CompilerParams(vmem_limit_bytes=VMEM_BYTES),
        name="data_part",
    )(
        slot, seen, albedo, *shots,
        obs_x, obs_x, obs_x, fit_x, fit_x, fit_x, obs_y, obs_y, obs_y, fit_y, fit_y, fit_y,
        surface_all,
    )


def update_kernel(rows, cols, me, center, up, down, left, right, data, out):
    g_up, g_down, g_left, g_right = edges(me[0], rows, cols)
    surface = center[0]
    above, below, before, after = shifted(
        surface,
        up[0, 7:8, :] * g_up,
        down[0, 0:1, :] * g_down,
        left[0, :, 127:128] * g_left,
        right[0, :, 0:1] * g_right,
    )
    laplace = below + above + after + before - 4.0 * surface
    out[...] = surface - step_size * (data[...].astype(jnp.float32) - smooth_weight * laplace)


def update(rows, cols, me, surface_all, data):
    side = data.shape[0]
    whole = pl.BlockSpec((side, side), lambda i, me: (0, 0))
    return pl.pallas_call(
        functools.partial(update_kernel, rows, cols),
        out_shape=jax.ShapeDtypeStruct((side, side), jnp.float32),
        grid_spec=pltpu.PrefetchScalarGridSpec(
            num_scalar_prefetch=1,
            grid=(1,),
            in_specs=rim_specs(side, cols, rows * cols, lambda i, me: me[0]) + [whole],
            out_specs=whole,
        ),
        compiler_params=pltpu.CompilerParams(vmem_limit_bytes=VMEM_BYTES),
        name="update",
    )(me, *([surface_all] * 5), data)


def total_kernel(rows, cols, part, total, held, send_sem, recv_sem):
    devices = rows * cols
    me = lax.axis_index("row") * cols + lax.axis_index("col")
    barrier = pltpu.get_barrier_semaphore()

    def place(step):
        peer = lax.rem(me + step, devices)
        return peer, (peer // cols, lax.rem(peer, cols))

    def greet(step, carry):
        unused, device = place(step)
        pl.semaphore_signal(barrier, inc=1, device_id=device, device_id_type=pl.DeviceIdType.MESH)
        return carry

    lax.fori_loop(1, devices, greet, 0)
    pl.semaphore_wait(barrier, devices - 1)

    def copy(step):
        unused, device = place(step)
        return pltpu.make_async_remote_copy(
            src_ref=part,
            dst_ref=held.at[step],
            send_sem=send_sem.at[step],
            recv_sem=recv_sem.at[step],
            device_id=device,
            device_id_type=pl.DeviceIdType.MESH,
        )

    def send(step, carry):
        copy(step).start()
        return carry

    def land(step, carry):
        copy(step).wait()
        return carry

    held[0] = part[...]
    lax.fori_loop(1, devices, send, 0)
    lax.fori_loop(1, devices, land, 0)
    sums = jnp.sum(held[...], axis=0)
    total[...] = jnp.full(total.shape, jnp.sum(sums[:8]) / jnp.sum(sums[8:]), jnp.float32)


def total_over_devices(rows, cols, part):
    devices = rows * cols
    return pl.pallas_call(
        functools.partial(total_kernel, rows, cols),
        out_shape=jax.ShapeDtypeStruct((8, 128), jnp.float32),
        in_specs=[pl.BlockSpec(memory_space=pltpu.VMEM)],
        out_specs=pl.BlockSpec(memory_space=pltpu.VMEM),
        scratch_shapes=[
            pltpu.VMEM((devices,) + part.shape, jnp.float32),
            pltpu.SemaphoreType.DMA((devices,)),
            pltpu.SemaphoreType.DMA((devices,)),
        ],
        compiler_params=pltpu.CompilerParams(
            collective_id=0, has_side_effects=True, vmem_limit_bytes=VMEM_BYTES
        ),
        name="total",
    )(part)


def add_kernel(
    rows, cols, data, out,
    own, got1, send2, got2, send3, got3, send4, got4,
    load_sem, ss1, rs1, ss2, rs2, ss3, rs3, ss4, rs4,
):
    X, Z = rows // 2, cols // 2
    side = out.shape[0]
    r, c = lax.axis_index("row"), lax.axis_index("col")
    x, k, z, y = r // 2, lax.rem(r, 2), c // 2, lax.rem(c, 2)
    core_peer = (x * 2 + 1 - k, c)
    y_peer = (r, z * 2 + 1 - y)
    x_at = [lax.rem(x + d, X) for d in range(X)]
    z_at = [lax.rem(z + e + 1, Z) for e in range(Z)]
    x_peers = [None] + [(x_at[d] * 2 + k, c) for d in range(1, X)]
    z_peers = [(r, z_at[e] * 2 + y) for e in range(Z - 1)]

    barrier = pltpu.get_barrier_semaphore()
    peers = [core_peer, y_peer] + x_peers[1:] + z_peers
    for peer in peers:
        pl.semaphore_signal(barrier, inc=1, device_id=peer, device_id_type=pl.DeviceIdType.MESH)
    pl.semaphore_wait(barrier, len(peers))

    def remote(src, dst, send, recv, peer):
        return pltpu.make_async_remote_copy(
            src_ref=src, dst_ref=dst, send_sem=send, recv_sem=recv,
            device_id=peer, device_id_type=pl.DeviceIdType.MESH,
        )

    first = [
        remote(data.at[:, 1 - k, z_at[e]], got1.at[e], ss1.at[e], rs1.at[e], core_peer)
        for e in range(Z)
    ]
    loads = [
        pltpu.make_async_copy(data.at[:, k, z_at[e]], own.at[e], load_sem.at[e]) for e in range(Z)
    ]
    second = [
        [
            remote(send2.at[e, d - 1], got2.at[e, d - 1], ss2.at[e, d - 1], rs2.at[e, d - 1], x_peers[d])
            for d in range(1, X)
        ]
        for e in range(Z)
    ]
    third = [remote(send3.at[e], got3.at[e], ss3.at[e], rs3.at[e], y_peer) for e in range(Z)]
    fourth = [
        remote(send4.at[e], got4.at[e], ss4.at[e], rs4.at[e], z_peers[e]) for e in range(Z - 1)
    ]
    for e in range(Z):
        first[e].start()
        loads[e].start()

    def by_rows(work):
        def step(j, carry):
            work(pl.ds(pl.multiple_of(j * 32, 32), 32))
            return carry

        lax.fori_loop(0, side // 32, step, 0)

    def over_x(e, which, at):
        total = own[e, x, which, at, :] + got1[e, x, which, at, :]
        for d in range(1, X):
            total = total + got2[e, d - 1, which, at, :].astype(jnp.float32)
        return total

    def stage2(e):
        loads[e].wait()
        first[e].wait_recv()
        for d in range(1, X):

            def work(at):
                for which in range(2):
                    total = own[e, x_at[d], which, at, :] + got1[e, x_at[d], which, at, :]
                    send2[e, d - 1, which, at, :] = total.astype(LINK)

            by_rows(work)
            second[e][d - 1].start()

    def stage3(e):
        for copy in second[e]:
            copy.wait_recv()

        def work(at):
            send3[e, at, :] = over_x(e, 1 - y, at).astype(LINK)

        by_rows(work)
        third[e].start()

    def stage4(e):
        third[e].wait_recv()

        def work(at):
            total = over_x(e, y, at) + got3[e, at, :].astype(jnp.float32)
            if e < Z - 1:
                send4[e, at, :] = total.astype(LINK)
            else:
                out[at, :] = total

        by_rows(work)
        if e < Z - 1:
            fourth[e].start()

    for t in range(Z + 2):
        if t < Z:
            stage2(t)
        if 0 <= t - 1 < Z:
            stage3(t - 1)
        if 0 <= t - 2 < Z:
            stage4(t - 2)
    for copy in fourth:
        copy.wait_recv()

    def finish(at):
        total = out[at, :]
        for e in range(Z - 1):
            total = total + got4[e, at, :].astype(jnp.float32)
        out[at, :] = total

    by_rows(finish)
    for copy in first + [one for some in second for one in some] + third + fourth:
        copy.wait_send()


def add_parts(rows, cols, data):
    X, Z = rows // 2, cols // 2
    side = data.shape[-1]
    vmem = lambda shape, dtype: pltpu.VMEM(shape + (side, side), dtype)
    dma = pltpu.SemaphoreType.DMA
    return pl.pallas_call(
        functools.partial(add_kernel, rows, cols),
        out_shape=jax.ShapeDtypeStruct((side, side), jnp.float32),
        in_specs=[pl.BlockSpec(memory_space=pl.ANY)],
        out_specs=pl.BlockSpec(memory_space=pltpu.VMEM),
        scratch_shapes=[
            vmem((Z, X, 2), jnp.float32),
            vmem((Z, X, 2), jnp.float32),
            vmem((Z, X - 1, 2), LINK),
            vmem((Z, X - 1, 2), LINK),
            vmem((Z,), LINK),
            vmem((Z,), LINK),
            vmem((Z - 1,), LINK),
            vmem((Z - 1,), LINK),
            dma((Z,)),
            dma((Z,)),
            dma((Z,)),
            dma((Z, X - 1)),
            dma((Z, X - 1)),
            dma((Z,)),
            dma((Z,)),
            dma((Z - 1,)),
            dma((Z - 1,)),
        ],
        compiler_params=pltpu.CompilerParams(
            collective_id=1, has_side_effects=True, vmem_limit_bytes=VMEM_BYTES
        ),
        name="add_parts",
    )(data.reshape(X, 2, Z, 2, side, side))


def gather_kernel(rows, cols, count, *refs):
    mine, outs = refs[:count], refs[count : 2 * count]
    local_sem, sz, rz, sa, ra, sb, rb, sc, rc = refs[2 * count :]
    X, Z = rows // 2, cols // 2
    side = mine[0].shape[0]
    half = side // 2
    r, c = lax.axis_index("row"), lax.axis_index("col")
    x, k, z, y = r // 2, lax.rem(r, 2), c // 2, lax.rem(c, 2)
    core_peer = (x * 2 + 1 - k, c)
    x_peers = [(lax.rem(x + d, X) * 2 + k, c) for d in range(1, X)]
    y_peers = [(r, z * 2 + 1 - y)]
    z_peers = [(r, lax.rem(z + d, Z) * 2 + y) for d in range(1, Z)]
    source = [lax.rem(z + Z - d, Z) for d in range(Z)]

    barrier = pltpu.get_barrier_semaphore()
    peers = [core_peer] + x_peers + y_peers + z_peers
    for peer in peers:
        pl.semaphore_signal(barrier, inc=1, device_id=peer, device_id_type=pl.DeviceIdType.MESH)
    pl.semaphore_wait(barrier, len(peers))

    def remote(src, dst, send, recv, peer):
        return pltpu.make_async_remote_copy(
            src_ref=src, dst_ref=dst, send_sem=send, recv_sem=recv,
            device_id=peer, device_id_type=pl.DeviceIdType.MESH,
        )

    own = [pltpu.make_async_copy(mine[n], outs[n].at[x, k, z, y], local_sem.at[n]) for n in range(count)]
    streams = []
    for n in range(count):
        own[n].start()
        for h in range(2):
            part = pl.ds(h * half, half)
            s = 2 * n + h
            along_z = [
                remote(
                    mine[n].at[part], outs[n].at[x, k, z, y, part],
                    sz.at[s, d], rz.at[s, d], z_peers[d],
                )
                for d in range(Z - 1)
            ]
            a_peers, b_peers = (x_peers, y_peers) if h else (y_peers, x_peers)
            along_a, along_b, along_core = [], [], []
            for e in range(Z):
                tile = outs[n].at[x, k, source[e], y, part]
                slab = outs[n].at[:, k, source[e], y, part] if h else outs[n].at[x, k, source[e], :, part]
                full = outs[n].at[:, k, source[e], :, part]
                along_a.append(
                    [
                        remote(tile, tile, sa.at[s, e, d], ra.at[s, e, d], peer)
                        for d, peer in enumerate(a_peers)
                    ]
                )
                along_b.append(
                    [
                        remote(slab, slab, sb.at[s, e, d], rb.at[s, e, d], peer)
                        for d, peer in enumerate(b_peers)
                    ]
                )
                along_core.append(remote(full, full, sc.at[s, e], rc.at[s, e], core_peer))
            for copy in along_z:
                copy.start()
            streams.append((along_z, along_a, along_b, along_core))
    for copy in own:
        copy.wait()
    for t in range(Z + 2):
        for along_z, along_a, along_b, along_core in streams:
            if t < Z:
                if t:
                    along_z[t - 1].wait_recv()
                for copy in along_a[t]:
                    copy.start()
            if 0 <= t - 1 < Z:
                for copy in along_a[t - 1]:
                    copy.wait_recv()
                for copy in along_b[t - 1]:
                    copy.start()
            if 0 <= t - 2 < Z:
                for copy in along_b[t - 2]:
                    copy.wait_recv()
                along_core[t - 2].start()
    for along_z, along_a, along_b, along_core in streams:
        for copy in along_core:
            copy.wait_recv()
        for copy in along_z + sum(along_a, []) + sum(along_b, []) + along_core:
            copy.wait_send()


def gather(rows, cols, values, collective):
    X, Z = rows // 2, cols // 2
    count, most = len(values), max(X - 1, 1)
    side = values[0].shape[0]
    anywhere = pl.BlockSpec(memory_space=pl.ANY)
    dma = pltpu.SemaphoreType.DMA
    streams = 2 * count
    outs = pl.pallas_call(
        functools.partial(gather_kernel, rows, cols, count),
        out_shape=[jax.ShapeDtypeStruct((X, 2, Z, 2, side, side), v.dtype) for v in values],
        in_specs=[anywhere] * count,
        out_specs=[anywhere] * count,
        scratch_shapes=[dma((count,))]
        + [dma((streams, Z - 1))] * 2
        + [dma((streams, Z, most))] * 4
        + [dma((streams, Z))] * 2,
        compiler_params=pltpu.CompilerParams(
            collective_id=collective, has_side_effects=True, vmem_limit_bytes=VMEM_BYTES
        ),
        name="gather",
    )(*values)
    return [out.reshape(rows * cols, side, side) for out in outs]


def image_plan(dest, tiles):
    count = dest.shape[0]
    place = jnp.arange(count)
    earlier = (dest[None, :] < dest[:, None]) | (
        (dest[None, :] == dest[:, None]) & (place[None, :] < place[:, None])
    )
    rank = jnp.sum(earlier, axis=1)
    chosen = rank[None, :] == place[:, None]
    order = jnp.sum(jnp.where(chosen, place[None, :], 0), axis=1).astype(jnp.int32)
    seen = jnp.any(dest[None, :] == jnp.arange(tiles)[:, None], axis=1)
    before = jnp.arange(tiles)[None, :] < jnp.arange(tiles)[:, None]
    tile_slot = jnp.where(seen, jnp.sum(before & seen[None, :], axis=1), 0).astype(jnp.int32)
    slots = jnp.arange(min(tiles, count) + 1)
    held = seen[None, :] & (tile_slot[None, :] == slots[:-1, None])
    slot_tile = jnp.sum(jnp.where(held, jnp.arange(tiles)[None, :], 0), axis=1).astype(jnp.int32)
    named = jnp.sum(dest[None, :] == jnp.arange(tiles)[:, None], axis=1)
    past = seen[None, :] & (tile_slot[None, :] < slots[:, None])
    start = jnp.sum(jnp.where(past, named[None, :], 0), axis=1).astype(jnp.int32)
    return (order, slot_tile, start), tile_slot, seen.astype(jnp.int32)


def shot_plan(dest, pixel, height, tiles):
    place = jnp.arange(dest.shape[0])
    earlier = (dest[None, :] < dest[:, None]) | (
        (dest[None, :] == dest[:, None]) & (place[None, :] < place[:, None])
    )
    rank = jnp.sum(earlier, axis=1)
    chosen = rank[None, :] == place[:, None]
    pixel = jnp.sum(jnp.where(chosen, pixel[None, :], 0), axis=1).astype(jnp.int32)
    height = jnp.sum(jnp.where(chosen, height[None, :], 0.0), axis=1)
    start = jnp.sum(dest[None, :] < jnp.arange(tiles + 1)[:, None], axis=1).astype(jnp.int32)
    return start, pixel, height


def body(heights, shadow, image_tiles, image_dest, sun_gain, shot_dest, shot_pixel, shot_height):
    rows, cols = lax.axis_size("row"), lax.axis_size("col")
    tiles = rows * cols
    side = heights.shape[0]
    me = (lax.axis_index("row") * cols + lax.axis_index("col")).astype(jnp.int32).reshape(1)
    plan, tile_slot, seen = image_plan(image_dest[:, 0], tiles)
    sun = sun_gain.astype(jnp.float32).reshape(-1)
    lit = (1 - shadow).astype(jnp.bfloat16)
    shots = shot_plan(shot_dest[:, 0], shot_pixel, shot_height, tiles)
    surface = heights
    for sweep in range(ITERS):
        if sweep == 0:
            surface_all, lit_all = gather(rows, cols, [surface, lit], 2)
        else:
            (surface_all,) = gather(rows, cols, [surface], 3)
        obs_x, obs_y, fit_x, fit_y, part = image_sums(
            rows, cols, plan, sun, image_tiles, surface_all, lit_all
        )
        albedo = total_over_devices(rows, cols, part)[0, :1]
        data = data_part(
            rows, cols, tile_slot, seen, albedo, shots, surface_all, obs_x, obs_y, fit_x, fit_y
        )
        data = add_parts(rows, cols, data)
        surface = update(rows, cols, me, surface_all, data)
    return surface


def solution(mesh):
    placed = (
        P("row", "col"),
        P("row", "col"),
        P(("row", "col"), None, None),
        P(("row", "col"), None),
        P(("row", "col"), None),
        P(("row", "col"), None),
        P(("row", "col")),
        P(("row", "col")),
    )
    return jax.shard_map(
        body, mesh=mesh, in_specs=placed, out_specs=P("row", "col"), check_vma=False
    )
```

```python
import functools
import math

import jax
import jax.numpy as jnp
from jax import lax
from jax.experimental import pallas as pl
from jax.experimental.pallas import tpu as pltpu
from jax.sharding import PartitionSpec as P

ITERS = 2

sharpness = 8.0
step_size = 0.01
smooth_weight = 2.0
laser_weight = 20.0

AXES = ("row", "col")
LOG2E = math.log2(math.e)
CHUNK = 16
LINK = jnp.bfloat16
VMEM_BYTES = 60 * 2**20


def rim_specs(side, cols, tiles, tile_of, high=8):
    def at(offset, block, where):
        def index(*args):
            tile = jnp.clip(tile_of(*args) + offset, 0, tiles - 1)
            return (tile,) + where

        return pl.BlockSpec((1,) + block, index)

    return [
        at(0, (side, side), (0, 0)),
        at(-cols, (high, side), (side // high - 1, 0)),
        at(cols, (high, side), (0, 0)),
        at(-1, (side, 128), (0, side // 128 - 1)),
        at(1, (side, 128), (0, 0)),
    ]


def edges(tile, rows, cols):
    row, col = tile // cols, lax.rem(tile, cols)
    as_gate = lambda test: jnp.where(test, 1.0, 0.0).astype(jnp.float32)
    return as_gate(row > 0), as_gate(row < rows - 1), as_gate(col > 0), as_gate(col < cols - 1)


def shifted(center, up, down, left, right):
    side = center.shape[0]
    row = lax.broadcasted_iota(jnp.int32, center.shape, 0)
    col = lax.broadcasted_iota(jnp.int32, center.shape, 1)
    above = jnp.where(row == 0, up, pltpu.roll(center, 1, 0))
    below = jnp.where(row == side - 1, down, pltpu.roll(center, side - 1, 0))
    before = jnp.where(col == 0, left, pltpu.roll(center, 1, 1))
    after = jnp.where(col == side - 1, right, pltpu.roll(center, side - 1, 1))
    return above, below, before, after


def image_kernel(
    rows, cols, order, tile, start, sun,
    pixels, center, up, down, left, right, lit,
    obs_x, obs_y, fit_x, fit_y, part,
    inv_s, px_s, py_s, ox_s, oy_s, fx_s, fy_s, cross, power,
):
    i = pl.program_id(0)
    side = center.shape[1]

    @pl.when(i == 0)
    def start_sums():
        cross[...] = jnp.zeros_like(cross)
        power[...] = jnp.zeros_like(power)

    @pl.when(start[i + 1] > start[i])
    def start_tile():
        g_up, g_down, g_left, g_right = edges(tile[i], rows, cols)
        above, below, before, after = shifted(
            center[0],
            up[0, 7:8, :] * g_up,
            down[0, 0:1, :] * g_down,
            left[0, :, 127:128] * g_left,
            right[0, :, 0:1] * g_right,
        )
        slope_x = (after - before) * 0.5
        slope_y = (below - above) * 0.5
        inverse = lax.rsqrt(1.0 + slope_x * slope_x + slope_y * slope_y)
        inv_s[...] = inverse
        px_s[...] = slope_x * inverse
        py_s[...] = slope_y * inverse

    def step(fresh, numbers, j, sums):
        k, ux, uy, uz, refl_scale, gx, gy, gc = numbers
        at = pl.ds(pl.multiple_of(j * CHUNK, CHUNK), CHUNK)
        inverse, px, py = inv_s[at, :], px_s[at, :], py_s[at, :]
        observed = pixels[k, at, :].astype(jnp.float32)
        shine = lit[0, at, :].astype(jnp.float32)
        u = uz * inverse - ux * px - uy * py
        soft = jnp.log2(1.0 + jnp.exp2(u))
        sigma = 1.0 - jnp.exp2(-soft)
        q = soft * refl_scale
        v = u * gc
        dx = gx + v * px
        dy = gy + v * py
        seen = sigma * observed
        model = sigma * q
        for held, term in (
            (ox_s, seen * dx), (oy_s, seen * dy), (fx_s, model * dx), (fy_s, model * dy)
        ):
            held[at, :] = term if fresh else held[at, :] + term
        shone = shine * q
        return sums[0] + shone * observed, sums[1] + shone * q

    def sweep(fresh, n):
        k = order[n]
        sx, sy, sz, gain = sun[4 * k], sun[4 * k + 1], sun[4 * k + 2], sun[4 * k + 3]
        scale = sharpness * LOG2E
        numbers = (
            k, sx * scale, sy * scale, sz * scale,
            gain * (1.0 / scale), gain * sx, gain * sy, gain * (1.0 / scale),
        )
        zero = jnp.zeros((CHUNK, side), jnp.float32)
        sums = lax.fori_loop(
            0, side // CHUNK, functools.partial(step, fresh, numbers), (zero, zero), unroll=8
        )
        cross[...] += sums[0]
        power[...] += sums[1]

    def more(n, carry):
        sweep(False, n)
        return carry

    pl.when(start[i + 1] > start[i])(lambda: sweep(True, start[i]))
    lax.fori_loop(start[i] + 1, start[i + 1], more, 0)

    @pl.when(start[i + 1] > start[i])
    def end_tile():
        factor = inv_s[...] * (-lit[0].astype(jnp.float32))
        obs_x[0] = (ox_s[...] * factor).astype(obs_x.dtype)
        obs_y[0] = (oy_s[...] * factor).astype(obs_y.dtype)
        fit_x[0] = (fx_s[...] * factor).astype(fit_x.dtype)
        fit_y[0] = (fy_s[...] * factor).astype(fit_y.dtype)

    @pl.when(i == pl.num_programs(0) - 1)
    def end_sums():
        for n, held in enumerate((cross, power)):
            total = jnp.zeros((8, 128), jnp.float32)
            for a in range(CHUNK // 8):
                for b in range(side // 128):
                    total = total + held[8 * a : 8 * a + 8, 128 * b : 128 * b + 128]
            part[8 * n : 8 * n + 8, :] = total


def image_sums(rows, cols, plan, sun, pixels, surface_all, lit_all):
    order, tile, start = plan
    images, side = pixels.shape[0], pixels.shape[1]
    tiles = rows * cols
    slots = min(tiles, images)
    by_tile = lambda i, order, tile, *rest: tile[i]
    field = jax.ShapeDtypeStruct((slots, side, side), jnp.bfloat16)
    part = jax.ShapeDtypeStruct((16, 128), jnp.float32)
    field_spec = pl.BlockSpec((1, side, side), lambda i, *rest: (i, 0, 0))
    part_spec = pl.BlockSpec((16, 128), lambda i, *rest: (0, 0))
    return pl.pallas_call(
        functools.partial(image_kernel, rows, cols),
        out_shape=[field] * 4 + [part],
        grid_spec=pltpu.PrefetchScalarGridSpec(
            num_scalar_prefetch=4,
            grid=(slots,),
            in_specs=[pl.BlockSpec(memory_space=pltpu.VMEM)]
            + rim_specs(side, cols, tiles, by_tile)
            + [pl.BlockSpec((1, side, side), lambda i, order, tile, *rest: (tile[i], 0, 0))],
            out_specs=[field_spec] * 4 + [part_spec],
            scratch_shapes=[pltpu.VMEM((side, side), jnp.float32)] * 7
            + [pltpu.VMEM((CHUNK, side), jnp.float32)] * 2,
        ),
        compiler_params=pltpu.CompilerParams(vmem_limit_bytes=VMEM_BYTES),
        name="image_sums",
    )(order, tile, start, sun, pixels, *([surface_all] * 5), lit_all)


def data_kernel(
    rows, cols, slot, seen, albedo, shot_start, shot_pixel, shot_height,
    ox, ox_l, ox_r, fx, fx_l, fx_r, oy, oy_u, oy_d, fy, fy_u, fy_d, surface, out,
):
    t = pl.program_id(0)
    tiles = rows * cols
    g_up, g_down, g_left, g_right = edges(t, rows, cols)
    a = albedo[0]
    has = lambda n: jnp.where(seen[jnp.clip(n, 0, tiles - 1)] == 1, a, 0.0)
    here, above, below = has(t), has(t - cols) * g_up, has(t + cols) * g_down
    before, after = has(t - 1) * g_left, has(t + 1) * g_right
    mix = lambda f, o, gate: (a * f.astype(jnp.float32) - o.astype(jnp.float32)) * gate
    grad_x = mix(fx[0], ox[0], here)
    grad_y = mix(fy[0], oy[0], here)
    side = grad_x.shape[0]
    left = mix(fx_l[0], ox_l[0], before)[:, 127:128]
    right = mix(fx_r[0], ox_r[0], after)[:, 0:1]
    up = mix(fy_u[0], oy_u[0], above)[15:16, :]
    down = mix(fy_d[0], oy_d[0], below)[0:1, :]
    row = lax.broadcasted_iota(jnp.int32, grad_x.shape, 0)
    col = lax.broadcasted_iota(jnp.int32, grad_x.shape, 1)
    y_above = jnp.where(row == 0, up, pltpu.roll(grad_y, 1, 0))
    y_below = jnp.where(row == side - 1, down, pltpu.roll(grad_y, side - 1, 0))
    x_before = jnp.where(col == 0, left, pltpu.roll(grad_x, 1, 1))
    x_after = jnp.where(col == side - 1, right, pltpu.roll(grad_x, side - 1, 1))
    out[0] = (x_before - x_after) * 0.5 + (y_above - y_below) * 0.5
    lane = lax.broadcasted_iota(jnp.int32, (1, side), 1)

    def shot(n, carry):
        pixel = shot_pixel[n]
        at = pl.ds(pixel // side, 1)
        misfit = laser_weight * (surface[0, at, :] - shot_height[n])
        out[0, at, :] += jnp.where(lane == lax.rem(pixel, side), misfit, 0.0)
        return carry

    lax.fori_loop(shot_start[t], shot_start[t + 1], shot, 0)


def data_part(rows, cols, slot, seen, albedo, shots, surface_all, obs_x, obs_y, fit_x, fit_y):
    side = obs_x.shape[1]
    tiles = rows * cols
    center, up, down, left, right = rim_specs(side, cols, tiles, lambda t, *rest: t, 16)

    def through(spec):
        def index(t, slot, *rest):
            place = spec.index_map(t)
            return (slot[place[0]],) + place[1:]

        return pl.BlockSpec(spec.block_shape, index)

    center, up, down, left, right = map(through, (center, up, down, left, right))
    return pl.pallas_call(
        functools.partial(data_kernel, rows, cols),
        out_shape=jax.ShapeDtypeStruct((tiles, side, side), jnp.float32),
        grid_spec=pltpu.PrefetchScalarGridSpec(
            num_scalar_prefetch=6,
            grid=(tiles,),
            in_specs=[center, left, right] * 2
            + [center, up, down] * 2
            + [pl.BlockSpec((1, side, side), lambda t, *rest: (t, 0, 0))],
            out_specs=pl.BlockSpec((1, side, side), lambda t, *rest: (t, 0, 0)),
        ),
        compiler_params=pltpu.CompilerParams(vmem_limit_bytes=VMEM_BYTES),
        name="data_part",
    )(
        slot, seen, albedo, *shots,
        obs_x, obs_x, obs_x, fit_x, fit_x, fit_x, obs_y, obs_y, obs_y, fit_y, fit_y, fit_y,
        surface_all,
    )


def update_kernel(rows, cols, me, center, up, down, left, right, data, out):
    g_up, g_down, g_left, g_right = edges(me[0], rows, cols)
    surface = center[0]
    above, below, before, after = shifted(
        surface,
        up[0, 7:8, :] * g_up,
        down[0, 0:1, :] * g_down,
        left[0, :, 127:128] * g_left,
        right[0, :, 0:1] * g_right,
    )
    laplace = below + above + after + before - 4.0 * surface
    out[...] = surface - step_size * (data[...].astype(jnp.float32) - smooth_weight * laplace)


def update(rows, cols, me, surface_all, data):
    side = data.shape[0]
    whole = pl.BlockSpec((side, side), lambda i, me: (0, 0))
    return pl.pallas_call(
        functools.partial(update_kernel, rows, cols),
        out_shape=jax.ShapeDtypeStruct((side, side), jnp.float32),
        grid_spec=pltpu.PrefetchScalarGridSpec(
            num_scalar_prefetch=1,
            grid=(1,),
            in_specs=rim_specs(side, cols, rows * cols, lambda i, me: me[0]) + [whole],
            out_specs=whole,
        ),
        compiler_params=pltpu.CompilerParams(vmem_limit_bytes=VMEM_BYTES),
        name="update",
    )(me, *([surface_all] * 5), data)


def total_kernel(rows, cols, part, total, held, send_sem, recv_sem):
    devices = rows * cols
    me = lax.axis_index("row") * cols + lax.axis_index("col")
    barrier = pltpu.get_barrier_semaphore()

    def place(step):
        peer = lax.rem(me + step, devices)
        return peer, (peer // cols, lax.rem(peer, cols))

    def greet(step, carry):
        unused, device = place(step)
        pl.semaphore_signal(barrier, inc=1, device_id=device, device_id_type=pl.DeviceIdType.MESH)
        return carry

    lax.fori_loop(1, devices, greet, 0)
    pl.semaphore_wait(barrier, devices - 1)

    def copy(step):
        unused, device = place(step)
        return pltpu.make_async_remote_copy(
            src_ref=part,
            dst_ref=held.at[step],
            send_sem=send_sem.at[step],
            recv_sem=recv_sem.at[step],
            device_id=device,
            device_id_type=pl.DeviceIdType.MESH,
        )

    def send(step, carry):
        copy(step).start()
        return carry

    def land(step, carry):
        copy(step).wait()
        return carry

    held[0] = part[...]
    lax.fori_loop(1, devices, send, 0)
    lax.fori_loop(1, devices, land, 0)
    sums = jnp.sum(held[...], axis=0)
    total[...] = jnp.full(total.shape, jnp.sum(sums[:8]) / jnp.sum(sums[8:]), jnp.float32)


def total_over_devices(rows, cols, part):
    devices = rows * cols
    return pl.pallas_call(
        functools.partial(total_kernel, rows, cols),
        out_shape=jax.ShapeDtypeStruct((8, 128), jnp.float32),
        in_specs=[pl.BlockSpec(memory_space=pltpu.VMEM)],
        out_specs=pl.BlockSpec(memory_space=pltpu.VMEM),
        scratch_shapes=[
            pltpu.VMEM((devices,) + part.shape, jnp.float32),
            pltpu.SemaphoreType.DMA((devices,)),
            pltpu.SemaphoreType.DMA((devices,)),
        ],
        compiler_params=pltpu.CompilerParams(
            collective_id=0, has_side_effects=True, vmem_limit_bytes=VMEM_BYTES
        ),
        name="total",
    )(part)


def add_kernel(
    rows, cols, data, out,
    own, got1, send2, got2, send3, got3, send4, got4,
    load_sem, ss1, rs1, ss2, rs2, ss3, rs3, ss4, rs4,
):
    X, Z = rows // 2, cols // 2
    side = out.shape[0]
    r, c = lax.axis_index("row"), lax.axis_index("col")
    x, k, z, y = r // 2, lax.rem(r, 2), c // 2, lax.rem(c, 2)
    core_peer = (x * 2 + 1 - k, c)
    y_peer = (r, z * 2 + 1 - y)
    x_at = [lax.rem(x + d, X) for d in range(X)]
    z_at = [lax.rem(z + e + 1, Z) for e in range(Z)]
    x_peers = [None] + [(x_at[d] * 2 + k, c) for d in range(1, X)]
    z_peers = [(r, z_at[e] * 2 + y) for e in range(Z - 1)]

    barrier = pltpu.get_barrier_semaphore()
    peers = [core_peer, y_peer] + x_peers[1:] + z_peers
    for peer in peers:
        pl.semaphore_signal(barrier, inc=1, device_id=peer, device_id_type=pl.DeviceIdType.MESH)
    pl.semaphore_wait(barrier, len(peers))

    def remote(src, dst, send, recv, peer):
        return pltpu.make_async_remote_copy(
            src_ref=src, dst_ref=dst, send_sem=send, recv_sem=recv,
            device_id=peer, device_id_type=pl.DeviceIdType.MESH,
        )

    first = [
        remote(data.at[:, 1 - k, z_at[e]], got1.at[e], ss1.at[e], rs1.at[e], core_peer)
        for e in range(Z)
    ]
    loads = [
        pltpu.make_async_copy(data.at[:, k, z_at[e]], own.at[e], load_sem.at[e]) for e in range(Z)
    ]
    second = [
        [
            remote(send2.at[e, d - 1], got2.at[e, d - 1], ss2.at[e, d - 1], rs2.at[e, d - 1], x_peers[d])
            for d in range(1, X)
        ]
        for e in range(Z)
    ]
    third = [remote(send3.at[e], got3.at[e], ss3.at[e], rs3.at[e], y_peer) for e in range(Z)]
    fourth = [
        remote(send4.at[e], got4.at[e], ss4.at[e], rs4.at[e], z_peers[e]) for e in range(Z - 1)
    ]
    for e in range(Z):
        first[e].start()
        loads[e].start()

    def by_rows(work):
        def step(j, carry):
            work(pl.ds(pl.multiple_of(j * 32, 32), 32))
            return carry

        lax.fori_loop(0, side // 32, step, 0)

    def over_x(e, which, at):
        total = own[e, x, which, at, :] + got1[e, x, which, at, :]
        for d in range(1, X):
            total = total + got2[e, d - 1, which, at, :].astype(jnp.float32)
        return total

    def stage2(e):
        loads[e].wait()
        first[e].wait_recv()
        for d in range(1, X):

            def work(at):
                for which in range(2):
                    total = own[e, x_at[d], which, at, :] + got1[e, x_at[d], which, at, :]
                    send2[e, d - 1, which, at, :] = total.astype(LINK)

            by_rows(work)
            second[e][d - 1].start()

    def stage3(e):
        for copy in second[e]:
            copy.wait_recv()

        def work(at):
            send3[e, at, :] = over_x(e, 1 - y, at).astype(LINK)

        by_rows(work)
        third[e].start()

    def stage4(e):
        third[e].wait_recv()

        def work(at):
            total = over_x(e, y, at) + got3[e, at, :].astype(jnp.float32)
            if e < Z - 1:
                send4[e, at, :] = total.astype(LINK)
            else:
                out[at, :] = total

        by_rows(work)
        if e < Z - 1:
            fourth[e].start()

    for t in range(Z + 2):
        if t < Z:
            stage2(t)
        if 0 <= t - 1 < Z:
            stage3(t - 1)
        if 0 <= t - 2 < Z:
            stage4(t - 2)
    for copy in fourth:
        copy.wait_recv()

    def finish(at):
        total = out[at, :]
        for e in range(Z - 1):
            total = total + got4[e, at, :].astype(jnp.float32)
        out[at, :] = total

    by_rows(finish)
    for copy in first + [one for some in second for one in some] + third + fourth:
        copy.wait_send()


def add_parts(rows, cols, data):
    X, Z = rows // 2, cols // 2
    side = data.shape[-1]
    vmem = lambda shape, dtype: pltpu.VMEM(shape + (side, side), dtype)
    dma = pltpu.SemaphoreType.DMA
    return pl.pallas_call(
        functools.partial(add_kernel, rows, cols),
        out_shape=jax.ShapeDtypeStruct((side, side), jnp.float32),
        in_specs=[pl.BlockSpec(memory_space=pl.ANY)],
        out_specs=pl.BlockSpec(memory_space=pltpu.VMEM),
        scratch_shapes=[
            vmem((Z, X, 2), jnp.float32),
            vmem((Z, X, 2), jnp.float32),
            vmem((Z, X - 1, 2), LINK),
            vmem((Z, X - 1, 2), LINK),
            vmem((Z,), LINK),
            vmem((Z,), LINK),
            vmem((Z - 1,), LINK),
            vmem((Z - 1,), LINK),
            dma((Z,)),
            dma((Z,)),
            dma((Z,)),
            dma((Z, X - 1)),
            dma((Z, X - 1)),
            dma((Z,)),
            dma((Z,)),
            dma((Z - 1,)),
            dma((Z - 1,)),
        ],
        compiler_params=pltpu.CompilerParams(
            collective_id=1, has_side_effects=True, vmem_limit_bytes=VMEM_BYTES
        ),
        name="add_parts",
    )(data.reshape(X, 2, Z, 2, side, side))


def gather_kernel(rows, cols, count, *refs):
    mine, outs = refs[:count], refs[count : 2 * count]
    local_sem, sz, rz, sa, ra, sb, rb, sc, rc = refs[2 * count :]
    X, Z = rows // 2, cols // 2
    side = mine[0].shape[0]
    half = side // 2
    r, c = lax.axis_index("row"), lax.axis_index("col")
    x, k, z, y = r // 2, lax.rem(r, 2), c // 2, lax.rem(c, 2)
    core_peer = (x * 2 + 1 - k, c)
    x_peers = [(lax.rem(x + d, X) * 2 + k, c) for d in range(1, X)]
    y_peers = [(r, z * 2 + 1 - y)]
    z_peers = [(r, lax.rem(z + d, Z) * 2 + y) for d in range(1, Z)]
    source = [lax.rem(z + Z - d, Z) for d in range(Z)]

    barrier = pltpu.get_barrier_semaphore()
    peers = [core_peer] + x_peers + y_peers + z_peers
    for peer in peers:
        pl.semaphore_signal(barrier, inc=1, device_id=peer, device_id_type=pl.DeviceIdType.MESH)
    pl.semaphore_wait(barrier, len(peers))

    def remote(src, dst, send, recv, peer):
        return pltpu.make_async_remote_copy(
            src_ref=src, dst_ref=dst, send_sem=send, recv_sem=recv,
            device_id=peer, device_id_type=pl.DeviceIdType.MESH,
        )

    own = [pltpu.make_async_copy(mine[n], outs[n].at[x, k, z, y], local_sem.at[n]) for n in range(count)]
    streams = []
    for n in range(count):
        own[n].start()
        for h in range(2):
            part = pl.ds(h * half, half)
            s = 2 * n + h
            along_z = [
                remote(
                    mine[n].at[part], outs[n].at[x, k, z, y, part],
                    sz.at[s, d], rz.at[s, d], z_peers[d],
                )
                for d in range(Z - 1)
            ]
            a_peers, b_peers = (x_peers, y_peers) if h else (y_peers, x_peers)
            along_a, along_b, along_core = [], [], []
            for e in range(Z):
                tile = outs[n].at[x, k, source[e], y, part]
                slab = outs[n].at[:, k, source[e], y, part] if h else outs[n].at[x, k, source[e], :, part]
                full = outs[n].at[:, k, source[e], :, part]
                along_a.append(
                    [
                        remote(tile, tile, sa.at[s, e, d], ra.at[s, e, d], peer)
                        for d, peer in enumerate(a_peers)
                    ]
                )
                along_b.append(
                    [
                        remote(slab, slab, sb.at[s, e, d], rb.at[s, e, d], peer)
                        for d, peer in enumerate(b_peers)
                    ]
                )
                along_core.append(remote(full, full, sc.at[s, e], rc.at[s, e], core_peer))
            for copy in along_z:
                copy.start()
            streams.append((along_z, along_a, along_b, along_core))
    for copy in own:
        copy.wait()
    for t in range(Z + 2):
        for along_z, along_a, along_b, along_core in streams:
            if t < Z:
                if t:
                    along_z[t - 1].wait_recv()
                for copy in along_a[t]:
                    copy.start()
            if 0 <= t - 1 < Z:
                for copy in along_a[t - 1]:
                    copy.wait_recv()
                for copy in along_b[t - 1]:
                    copy.start()
            if 0 <= t - 2 < Z:
                for copy in along_b[t - 2]:
                    copy.wait_recv()
                along_core[t - 2].start()
    for along_z, along_a, along_b, along_core in streams:
        for copy in along_core:
            copy.wait_recv()
        for copy in along_z + sum(along_a, []) + sum(along_b, []) + along_core:
            copy.wait_send()


def gather(rows, cols, values, collective):
    X, Z = rows // 2, cols // 2
    count, most = len(values), max(X - 1, 1)
    side = values[0].shape[0]
    anywhere = pl.BlockSpec(memory_space=pl.ANY)
    dma = pltpu.SemaphoreType.DMA
    streams = 2 * count
    outs = pl.pallas_call(
        functools.partial(gather_kernel, rows, cols, count),
        out_shape=[jax.ShapeDtypeStruct((X, 2, Z, 2, side, side), v.dtype) for v in values],
        in_specs=[anywhere] * count,
        out_specs=[anywhere] * count,
        scratch_shapes=[dma((count,))]
        + [dma((streams, Z - 1))] * 2
        + [dma((streams, Z, most))] * 4
        + [dma((streams, Z))] * 2,
        compiler_params=pltpu.CompilerParams(
            collective_id=collective, has_side_effects=True, vmem_limit_bytes=VMEM_BYTES
        ),
        name="gather",
    )(*values)
    return [out.reshape(rows * cols, side, side) for out in outs]


def image_plan(dest, tiles):
    count = dest.shape[0]
    place = jnp.arange(count)
    earlier = (dest[None, :] < dest[:, None]) | (
        (dest[None, :] == dest[:, None]) & (place[None, :] < place[:, None])
    )
    rank = jnp.sum(earlier, axis=1)
    chosen = rank[None, :] == place[:, None]
    order = jnp.sum(jnp.where(chosen, place[None, :], 0), axis=1).astype(jnp.int32)
    seen = jnp.any(dest[None, :] == jnp.arange(tiles)[:, None], axis=1)
    before = jnp.arange(tiles)[None, :] < jnp.arange(tiles)[:, None]
    tile_slot = jnp.where(seen, jnp.sum(before & seen[None, :], axis=1), 0).astype(jnp.int32)
    slots = jnp.arange(min(tiles, count) + 1)
    held = seen[None, :] & (tile_slot[None, :] == slots[:-1, None])
    slot_tile = jnp.sum(jnp.where(held, jnp.arange(tiles)[None, :], 0), axis=1).astype(jnp.int32)
    named = jnp.sum(dest[None, :] == jnp.arange(tiles)[:, None], axis=1)
    past = seen[None, :] & (tile_slot[None, :] < slots[:, None])
    start = jnp.sum(jnp.where(past, named[None, :], 0), axis=1).astype(jnp.int32)
    return (order, slot_tile, start), tile_slot, seen.astype(jnp.int32)


def shot_plan(dest, pixel, height, tiles):
    place = jnp.arange(dest.shape[0])
    earlier = (dest[None, :] < dest[:, None]) | (
        (dest[None, :] == dest[:, None]) & (place[None, :] < place[:, None])
    )
    rank = jnp.sum(earlier, axis=1)
    chosen = rank[None, :] == place[:, None]
    pixel = jnp.sum(jnp.where(chosen, pixel[None, :], 0), axis=1).astype(jnp.int32)
    height = jnp.sum(jnp.where(chosen, height[None, :], 0.0), axis=1)
    start = jnp.sum(dest[None, :] < jnp.arange(tiles + 1)[:, None], axis=1).astype(jnp.int32)
    return start, pixel, height


def body(heights, shadow, image_tiles, image_dest, sun_gain, shot_dest, shot_pixel, shot_height):
    rows, cols = lax.axis_size("row"), lax.axis_size("col")
    tiles = rows * cols
    side = heights.shape[0]
    me = (lax.axis_index("row") * cols + lax.axis_index("col")).astype(jnp.int32).reshape(1)
    plan, tile_slot, seen = image_plan(image_dest[:, 0], tiles)
    sun = sun_gain.astype(jnp.float32).reshape(-1)
    lit = (1 - shadow).astype(jnp.bfloat16)
    shots = shot_plan(shot_dest[:, 0], shot_pixel, shot_height, tiles)
    surface = heights
    for sweep in range(ITERS):
        if sweep == 0:
            surface_all, lit_all = gather(rows, cols, [surface, lit], 2)
        else:
            (surface_all,) = gather(rows, cols, [surface], 3)
        obs_x, obs_y, fit_x, fit_y, part = image_sums(
            rows, cols, plan, sun, image_tiles, surface_all, lit_all
        )
        albedo = total_over_devices(rows, cols, part)[0, :1]
        data = data_part(
            rows, cols, tile_slot, seen, albedo, shots, surface_all, obs_x, obs_y, fit_x, fit_y
        )
        data = add_parts(rows, cols, data)
        surface = update(rows, cols, me, surface_all, data)
    return surface


def solution(mesh):
    placed = (
        P("row", "col"),
        P("row", "col"),
        P(("row", "col"), None, None),
        P(("row", "col"), None),
        P(("row", "col"), None),
        P(("row", "col"), None),
        P(("row", "col")),
        P(("row", "col")),
    )
    return jax.shard_map(
        body, mesh=mesh, in_specs=placed, out_specs=P("row", "col"), check_vma=False
    )
```
